256 devices in a mesh: batch: 2 (over core), ctx: 32 (over z, x), head: 4 (over y).
Axes of the slice: x: 4, y: 4, z: 8, core: 2. Of those that a mesh axis runs over, the one named last changes fastest.
Arguments:
- queries: bfloat16 [32768, 2048], P(('batch', 'ctx'), 'head'), parts along dimension 0, may hold values from -6 to 6
- key_value: bfloat16 [32768, 2, 2048], P(('batch', 'ctx'), None, 'head'), parts along dimension 0, may hold values from -6 to 6
- out_weight: bfloat16 [2048, 4096], P('head'), may hold values from -2 to 2
- random_blocks: int32 [512, 3], P('batch'), parts along dimension 0, may hold values from 0 to 255, as said below
- global_ids: int32 [4], P('batch'), parts along dimension 0, may hold values from 0 to 255, as said below
Outputs:
- projected: bfloat16 [32768, 4096], P(('batch', 'ctx'), 'head'), parts along dimension 0
The draws below stay inside these ranges and needn't reach their ends.
There are 2 independent parts, one for each index of `batch`. The reference program is written for one: setup_inputs(seed, part) draws one part's arguments, and reference() takes and returns one part's arrays. A program takes and returns all parts, laid end to end along the dimension named above; an argument that names none is the same for every part. Nothing has to cross between parts.
Inputs may be any that keep to these rules, and one draw needn't show every extreme that they name: `random_blocks`: row i lists random key blocks of query block i; entries may repeat. Among the 3 * 8 entries of the 8 aligned rows of one index of ctx, at most 2 lie in the blocks of any one index of ctx (blocks d * 8 to d * 8 + 7). In every draw there is one index of ctx, the same for all rows, whose blocks are named exactly 2 times by the rows of every index of ctx. `global_ids`: 2 distinct blocks; one of them is always the last block, 255, at a position drawn from the seed.
All inputs are finite; a program needn't handle non-finite values.
Results may differ from the reference program's by a relative error of at most 0.015.
Values may be sent and summed in bfloat16 or wider, within the bound.
No kernel may reach another device: no remote copies, remote signals or barrier semaphores. Data moves between devices by JAX's collectives and lax.ppermute only.
A program may use at most 128 MiB of HBM per device.

```python
import math
import jax
import jax.numpy as jnp
from jax import lax

D = 4096
HEADS = 16
DH = 128
BLK = 64
GLOB = 2
RAND = 3
HF = 2048
BPD = 8
SEQ = 16384
NB = 256
CAP = 2
N_CTX = 32


def draw_queries(key, part):
    result = jax.random.uniform(jax.random.fold_in(key, 41), (SEQ, HF), jnp.float32, -6.0, 6.0)
    return result.astype(jnp.bfloat16)


def draw_key_value(key, part):
    key_part = jax.random.uniform(jax.random.fold_in(key, 42), (SEQ, HF), jnp.float32, -6.0, 6.0)
    value_part = jax.random.truncated_normal(jax.random.fold_in(key, 43), -6.0, 6.0, (SEQ, HF), jnp.float32)
    result = jnp.stack([key_part, value_part], axis=1)
    return result.astype(jnp.bfloat16)


def draw_random_blocks(key, part):
    slots = RAND * BPD
    hot_owner = jax.random.randint(jax.random.fold_in(key, 11), (), 0, N_CTX)

    def per_device(device_key):
        shuffled = jax.random.permutation(jax.random.fold_in(device_key, 1), (N_CTX - 1) * CAP)[:slots - CAP]
        others = shuffled // CAP
        others = others + (others >= hot_owner).astype(jnp.int32)
        owners = jnp.concatenate([jnp.full((CAP,), hot_owner, jnp.int32), others.astype(jnp.int32)])
        reorder = jax.random.permutation(jax.random.fold_in(device_key, 2), slots)
        owners = owners[reorder]
        local_pick = jax.random.randint(jax.random.fold_in(device_key, 3), (slots,), 0, BPD)
        return (owners * BPD + local_pick).astype(jnp.int32)
    device_keys = jax.random.split(jax.random.fold_in(key, 12), N_CTX)
    table = jax.vmap(per_device)(device_keys)
    return table.reshape(NB, RAND)


def draw_global_ids(key, part):
    key = jax.random.fold_in(key, 21)
    chosen = jax.random.permutation(jax.random.fold_in(key, 1), NB - 1)[:GLOB - 1].astype(jnp.int32)
    listed = jnp.concatenate([chosen, jnp.full((1,), NB - 1, jnp.int32)])
    turn = jax.random.randint(jax.random.fold_in(key, 2), (), 0, GLOB)
    return jnp.roll(listed, turn).astype(jnp.int32)


def level_of(key, dims, shards, least, high):
    factor_of = 1.0
    for position, blocks in shards:
        heights = jax.random.uniform(jax.random.fold_in(jax.random.fold_in(key, 6), position), (blocks,), jnp.float32, least / len(shards), high / len(shards))
        factor_of = factor_of * jnp.repeat(jnp.exp(heights), dims[position] // blocks).reshape((-1,) + (1,) * (len(dims) - 1 - position))
    return factor_of


def gaussian(key, dims, scale, bound, pieces=(), held_as=jnp.bfloat16):
    array = jax.random.normal(key, dims, jnp.float32) * scale
    if len(pieces) > 0:
        array = level_of(key, dims, pieces, -0.22, 0.18) * array
    return jnp.clip(array, min=-bound, max=bound).astype(held_as)


def setup_inputs(seed: int = 0, part: int = 0) -> dict:
    keys = jax.random.split(jax.random.key(seed), 6)
    part_splits = jax.random.split(jax.random.fold_in(keys[5], part), 6)
    queries = draw_queries(jax.random.fold_in(jax.random.fold_in(keys[5], part), 71), part)
    key_value = draw_key_value(jax.random.fold_in(jax.random.fold_in(keys[5], part), 71), part)
    out_weight = gaussian(keys[2], (HF, D), (max(1, HF // 256)) ** -0.5, 2.0, ((0, 4),))
    random_blocks = draw_random_blocks(jax.random.fold_in(jax.random.fold_in(keys[5], part), 71), part)
    global_ids = draw_global_ids(jax.random.fold_in(jax.random.fold_in(keys[5], part), 71), part)
    return {"queries": queries, "key_value": key_value, "out_weight": out_weight, "random_blocks": random_blocks, "global_ids": global_ids}


def reference(queries, key_value, out_weight, random_blocks, global_ids):
    length = queries.shape[0]
    num_blocks = length // BLK
    score_scaling = 1.0 / math.sqrt(DH)
    glob_count = global_ids.shape[0]
    picks = random_blocks.shape[1]
    block_number = jnp.arange(num_blocks, dtype=jnp.int32)
    block_list = jnp.concatenate([(block_number - 1)[:, None], block_number[:, None], (block_number + 1)[:, None], jnp.broadcast_to(global_ids[None, :], (num_blocks, glob_count)).astype(jnp.int32), random_blocks.astype(jnp.int32)], axis=1)
    usable = jnp.concatenate([(block_number > 0)[:, None], jnp.ones((num_blocks, 1), bool), (block_number < num_blocks - 1)[:, None], jnp.ones((num_blocks, glob_count + picks), bool)], axis=1)
    block_list = jnp.clip(block_list, 0, num_blocks - 1).astype(jnp.int32)
    key_mask = jnp.repeat(usable, BLK, axis=1)
    listed_count = block_list.shape[1]
    keys_all = key_value[:, 0]
    values_all = key_value[:, 1]

    def per_head(head_index):
        start = head_index * DH
        q_head = lax.dynamic_slice_in_dim(queries, start, DH, 1).astype(jnp.float32)
        k_head = lax.dynamic_slice_in_dim(keys_all, start, DH, 1).astype(jnp.float32)
        v_head = lax.dynamic_slice_in_dim(values_all, start, DH, 1).astype(jnp.float32)
        query_blocks = q_head.reshape(num_blocks, BLK, DH)
        gathered_key_rows = k_head.reshape(num_blocks, BLK, DH)[block_list].reshape(num_blocks, listed_count * BLK, DH)
        gathered_value_rows = v_head.reshape(num_blocks, BLK, DH)[block_list].reshape(num_blocks, listed_count * BLK, DH)
        logit_scores = jnp.einsum('way,why->wah', query_blocks, gathered_key_rows) * score_scaling
        logit_scores = jnp.where(key_mask[:, None, :], logit_scores, -jnp.inf)
        row_max = lax.optimization_barrier(jnp.max(logit_scores, axis=-1, keepdims=True))
        weights = jnp.exp(logit_scores - row_max)
        softmax_totals = lax.optimization_barrier(jnp.sum(weights, axis=-1))
        rounded_scores = lax.optimization_barrier(weights.astype(jnp.bfloat16)).astype(jnp.float32)
        attended_values = jnp.einsum('onh,ohy->ony', rounded_scores, gathered_value_rows) / softmax_totals[..., None]
        glob_q = query_blocks[global_ids]
        glob_scores = jnp.einsum('gqd,kd->gqk', glob_q, k_head) * score_scaling
        glob_max = lax.optimization_barrier(jnp.max(glob_scores, axis=-1, keepdims=True))
        glob_weights = jnp.exp(glob_scores - glob_max)
        glob_totals = lax.optimization_barrier(jnp.sum(glob_weights, axis=-1))
        glob_out = jnp.einsum('gqk,kd->gqd', glob_weights, v_head, precision=lax.Precision.HIGHEST) / glob_totals[..., None]
        attended_values = attended_values.at[global_ids].set(glob_out)
        return attended_values.reshape(length, DH).astype(jnp.bfloat16)
    heads_out = lax.map(per_head, jnp.arange(HEADS, dtype=jnp.int32))
    attention = jnp.transpose(heads_out, (1, 0, 2)).reshape(length, HEADS * DH)
    return jnp.dot(attention, out_weight, preferred_element_type=jnp.float32).astype(jnp.bfloat16)
```

```python
import functools
import math

import jax
import jax.numpy as jnp
from jax import lax
from jax.experimental import pallas as pl
from jax.experimental.pallas import tpu as pltpu
from jax.sharding import Mesh
from jax.sharding import PartitionSpec as P

DH = 128
BLK = 64
NEG = -1e30
NZ = 8
NX = 4
NY = 4
BPD = 8
TOK = BLK * BPD
PAIR = 2
WIDE = PAIR * DH
STAT = 16
GROUP = 4
QBS = NX * BPD
SCALE = 1.0 / math.sqrt(DH)
VMEM = 48 * 1024 * 1024

any_space = pl.BlockSpec(memory_space=pl.ANY)
in_vmem = pl.BlockSpec(memory_space=pltpu.VMEM)
in_smem = pl.BlockSpec(memory_space=pltpu.SMEM)


def shift(count, by):
    return [(i, (i + by) % count) for i in range(count)]


def lists_kernel(table, glob, place, count, index, dense):
    z, x = place[0], place[1]
    for k in range(QBS * 8 + 8):
        index[k] = 0
    for g in range(2):
        owner = glob[g] >> 3
        slot = (x - (owner & 3)) & 3
        dense[g] = jnp.where((owner >> 2) == z, slot * BPD + (glob[g] & 7), -1)

    def one(qb, carry):
        qx = (x - (qb >> 3)) & 3
        block = ((z * NX + qx) << 3) + (qb & 7)
        entries = [(block - 1, block > 0), (block, None)]
        entries += [(block + 1, block < NZ * NX * BPD - 1)]
        entries += [(glob[0], None), (glob[1], None)]
        entries += [(table[block * 3 + j], None) for j in range(3)]
        filled = jnp.int32(0)
        for key, exists in entries:
            key = jnp.clip(key, 0, NZ * NX * BPD - 1)
            owner = key >> 3
            here = (owner & 3) == x
            if exists is not None:
                here = here & exists
            index[qb * 8 + filled] = ((((owner >> 2) - z) & 7) << 3) + (key & 7)
            filled = filled + here.astype(jnp.int32)
        is_global = (block == glob[0]) | (block == glob[1])
        count[qb] = jnp.where(is_global, 0, filled)
        return carry

    lax.fori_loop(0, QBS, one, 0)


def make_lists(table, glob, place):
    return pl.pallas_call(
        lists_kernel,
        out_shape=[
            jax.ShapeDtypeStruct((QBS,), jnp.int32),
            jax.ShapeDtypeStruct((QBS * 8 + 8,), jnp.int32),
            jax.ShapeDtypeStruct((2,), jnp.int32),
        ],
        in_specs=[in_smem] * 3,
        out_specs=[in_smem] * 3,
    )(table, glob, place)


def dot_t(a, b):
    return lax.dot_general(a, b, (((1,), (1,)), ((), ())), preferred_element_type=jnp.float32)


def attend_kernel(chunk, *refs):
    count, index, dense = refs[:3]
    q_in = refs[3:7]
    kv_in = refs[7:14]
    k_far, v_far = refs[14:16]
    out = refs[16:20]
    q_s, kv_s, o_s, stat, sems = refs[20:]
    copies = []
    for s in range(NX):
        copies.append((q_in[s].at[:, pl.ds(chunk * WIDE, WIDE)], q_s.at[s]))
    for p in range(7):
        copies.append((kv_in[p], kv_s.at[p if p < 4 else p + 1]))
    copies.append((k_far, kv_s.at[4, 0]))
    copies.append((v_far, kv_s.at[4, 1]))
    copies = [pltpu.make_async_copy(a, b, sems.at[n]) for n, (a, b) in enumerate(copies)]
    for copy in copies:
        copy.start()
    for copy in copies:
        copy.wait()

    def finish(slot, local, head, m, total, acc):
        safe = jnp.maximum(total, 1e-30)
        rows = pl.ds(pl.multiple_of(local * BLK, BLK), BLK)
        o_s[slot, rows, head * DH : (head + 1) * DH] = (acc / safe).astype(jnp.bfloat16)
        lse = jnp.where(total > 0.0, m + jnp.log(safe), NEG)
        stat[head, pl.ds(pl.multiple_of((slot * BPD + local) * BLK, BLK), BLK), :] = (
            jnp.broadcast_to(lse, (BLK, DH))
        )

    def load_q(slot, local, head):
        rows = pl.ds(pl.multiple_of(local * BLK, BLK), BLK)
        return q_s[slot, rows, head * DH : (head + 1) * DH]

    lane = lax.broadcasted_iota(jnp.int32, (BLK, 2 * BLK), 1)

    def group(g, carry):
        counts = [count[g * GROUP + i] for i in range(GROUP)]
        most = functools.reduce(jnp.maximum, counts)
        slot = g // (BPD // GROUP)
        first = (g % (BPD // GROUP)) * GROUP
        chains = [(i, h) for i in range(GROUP) for h in range(PAIR)]

        def step(t, state):
            out_state = []
            for n, (i, h) in enumerate(chains):
                m, total, acc = state[n]
                base = (g * GROUP + i) * 8 + 2 * t
                cols = slice(h * DH, (h + 1) * DH)
                keys, values = [], []
                for e in range(2):
                    entry = index[base + e]
                    piece = entry >> 3
                    rows = pl.ds(pl.multiple_of((entry & 7) * BLK, BLK), BLK)
                    keys.append(kv_s[piece, 0, rows, cols])
                    values.append(kv_s[piece, 1, rows, cols])
                keys = jnp.concatenate(keys, axis=0)
                values = jnp.concatenate(values, axis=0)
                live = lane < (counts[i] - 2 * t) * BLK
                scores = dot_t(load_q(slot, first + i, h), keys) * SCALE
                scores = jnp.where(live, scores, NEG)
                m_new = jnp.maximum(m, jnp.max(scores, axis=1, keepdims=True))
                weights = jnp.where(live, jnp.exp(scores - m_new), 0.0)
                keep = jnp.exp(m - m_new)
                total = total * keep + jnp.sum(weights, axis=1, keepdims=True)
                acc = acc * keep + jnp.dot(
                    weights.astype(jnp.bfloat16), values, preferred_element_type=jnp.float32
                )
                out_state.append((m_new, total, acc))
            return tuple(out_state)

        start = tuple(
            (
                jnp.full((BLK, 1), NEG, jnp.float32),
                jnp.zeros((BLK, 1), jnp.float32),
                jnp.zeros((BLK, DH), jnp.float32),
            )
            for _ in chains
        )
        state = lax.fori_loop(0, (most + 1) // 2, step, start)
        for (i, h), (m, total, acc) in zip(chains, state):
            finish(slot, first + i, h, m, total, acc)
        return carry

    lax.fori_loop(0, QBS // GROUP, group, 0)

    for g in range(2):

        @pl.when(dense[g] >= 0)
        def _(g=g):
            slot = dense[g] >> 3
            local = dense[g] & 7

            def step(p, state):
                out_state = []
                for h in range(PAIR):
                    m, total, acc = state[h]
                    cols = slice(h * DH, (h + 1) * DH)
                    scores = dot_t(load_q(slot, local, h), kv_s[p, 0, :, cols]) * SCALE
                    m_new = jnp.maximum(m, jnp.max(scores, axis=1, keepdims=True))
                    weights = jnp.exp(scores - m_new)
                    keep = jnp.exp(m - m_new)
                    total = total * keep + jnp.sum(weights, axis=1, keepdims=True)
                    acc = acc * keep + jnp.dot(
                        weights.astype(jnp.bfloat16),
                        kv_s[p, 1, :, cols],
                        preferred_element_type=jnp.float32,
                    )
                    out_state.append((m_new, total, acc))
                return tuple(out_state)

            start = tuple(
                (
                    jnp.full((BLK, 1), NEG, jnp.float32),
                    jnp.zeros((BLK, 1), jnp.float32),
                    jnp.zeros((BLK, DH), jnp.float32),
                )
                for _ in range(PAIR)
            )
            state = lax.fori_loop(0, NZ, step, start)
            for h in range(PAIR):
                finish(slot, local, h, *state[h])

    eye = lax.broadcasted_iota(jnp.int32, (DH, DH), 0) == lax.broadcasted_iota(
        jnp.int32, (DH, DH), 1
    )
    for s in range(NX):
        for h in range(PAIR):
            lines = []
            for t in range(TOK // DH):
                tile = stat[h, s * TOK + t * DH : s * TOK + (t + 1) * DH, :]
                lines.append(jnp.sum(jnp.where(eye, tile, 0.0), axis=0, keepdims=True))
            left = jnp.concatenate(lines, axis=0)
            terms = []
            for _ in range(3):
                term = left.astype(jnp.bfloat16).astype(jnp.float32)
                terms.append(term)
                left = left - term
            terms.append(jnp.zeros_like(left))
            o_s[s, TOK : TOK + STAT, h * DH : (h + 1) * DH] = jnp.concatenate(
                terms, axis=0
            ).astype(jnp.bfloat16)
    back = [pltpu.make_async_copy(o_s.at[s], out[s], sems.at[s]) for s in range(NX)]
    for copy in back:
        copy.start()
    for copy in back:
        copy.wait()


def attend(chunk, lists, queries, pieces, k_far, v_far):
    message = jax.ShapeDtypeStruct((TOK + STAT, WIDE), jnp.bfloat16)
    return pl.pallas_call(
        functools.partial(attend_kernel, chunk),
        out_shape=[message] * NX,
        in_specs=[in_smem] * 3 + [any_space] * 13,
        out_specs=[any_space] * NX,
        scratch_shapes=[
            pltpu.VMEM((NX, TOK, WIDE), jnp.bfloat16),
            pltpu.VMEM((NZ, 2, TOK, WIDE), jnp.bfloat16),
            pltpu.VMEM((NX, TOK + STAT, WIDE), jnp.bfloat16),
            pltpu.VMEM((PAIR, NX * TOK, DH), jnp.float32),
            pltpu.SemaphoreType.DMA((13,)),
        ],
        compiler_params=pltpu.CompilerParams(vmem_limit_bytes=VMEM),
        cost_estimate=pl.CostEstimate(
            flops=1_500_000_000, bytes_accessed=8_000_000, transcendentals=2_000_000
        ),
    )(*lists, *queries, *pieces, k_far, v_far)


def join_kernel(m0, m1, m2, m3, out):
    shares = (m0, m1, m2, m3)
    eye = lax.broadcasted_iota(jnp.int32, (DH, DH), 0) == lax.broadcasted_iota(
        jnp.int32, (DH, DH), 1
    )
    for h in range(PAIR):
        cols = slice(h * DH, (h + 1) * DH)
        stats = []
        for share in shares:
            terms = share[TOK : TOK + STAT, cols].astype(jnp.float32)
            stats.append(terms[0:4] + terms[4:8] + terms[8:12])
        for t in range(TOK // DH):
            lse = [
                jnp.sum(
                    jnp.where(eye, jnp.broadcast_to(s[t : t + 1], (DH, DH)), 0.0),
                    axis=1,
                    keepdims=True,
                )
                for s in stats
            ]
            top = functools.reduce(jnp.maximum, lse)
            scale = [jnp.exp(v - top) for v in lse]
            norm = functools.reduce(jnp.add, scale)
            rows = slice(t * DH, (t + 1) * DH)
            terms = [f * s[rows, cols].astype(jnp.float32) for f, s in zip(scale, shares)]
            out[rows, cols] = (functools.reduce(jnp.add, terms) / norm).astype(jnp.bfloat16)


def join(messages):
    return pl.pallas_call(
        join_kernel,
        out_shape=jax.ShapeDtypeStruct((TOK, WIDE), jnp.bfloat16),
        in_specs=[in_vmem] * NX,
        out_specs=in_vmem,
        compiler_params=pltpu.CompilerParams(vmem_limit_bytes=VMEM),
        cost_estimate=pl.CostEstimate(
            flops=4_000_000, bytes_accessed=1_300_000, transcendentals=8_000
        ),
    )(*messages)


def project_kernel(last, *refs):
    att, weight = refs[:NY], refs[NY : 2 * NY]
    total = functools.reduce(
        jnp.add,
        [jnp.dot(a[...], w[...], preferred_element_type=jnp.float32) for a, w in zip(att, weight)],
    )
    if last:
        total = total + refs[2 * NY][...]
    refs[-1][...] = total.astype(refs[-1].dtype)


def project(chunk, att, weight, so_far=None):
    last = so_far is not None
    columns = weight[0].shape[1]
    tile = 256
    out_spec = pl.BlockSpec((TOK, tile), lambda j: (0, j))
    return pl.pallas_call(
        functools.partial(project_kernel, last),
        grid=(columns // tile,),
        out_shape=jax.ShapeDtypeStruct((TOK, columns), jnp.bfloat16 if last else jnp.float32),
        in_specs=[pl.BlockSpec((TOK, WIDE), lambda j: (0, 0))] * NY
        + [pl.BlockSpec((WIDE, tile), lambda j: (chunk, j))] * NY
        + [out_spec] * last,
        out_specs=out_spec,
        compiler_params=pltpu.CompilerParams(vmem_limit_bytes=VMEM),
        cost_estimate=pl.CostEstimate(
            flops=1_073_741_824, bytes_accessed=5_000_000, transcendentals=0
        ),
    )(*att, *weight, *([so_far] if last else []))


def ring_step(right, left):
    return (
        lax.ppermute(right, "z", shift(NZ, 1)),
        lax.ppermute(left, "z", shift(NZ, -1)),
    )


def body(queries, key_value, out_weight, random_blocks, global_ids):
    z, x, y = lax.axis_index("z"), lax.axis_index("x"), lax.axis_index("head")
    split = jnp.transpose(key_value, (1, 0, 2))
    own = [split[:, :, c * WIDE : (c + 1) * WIDE] for c in range(2)]
    place = jnp.stack([z, x]).astype(jnp.int32)
    lists = make_lists(random_blocks.reshape(-1), global_ids, place)
    behind = [[own[c]] for c in range(2)]
    ahead = [[own[c]] for c in range(2)]
    for _ in range(3):
        for c in range(2):
            right, left = ring_step(behind[c][-1], ahead[c][-1])
            behind[c].append(right)
            ahead[c].append(left)
    far = [ring_step(behind[c][3][0], ahead[c][3][1]) for c in range(2)]
    all_queries = [queries] + [lax.ppermute(queries, "x", shift(NX, s)) for s in range(1, NX)]
    columns = out_weight.shape[1] // NY
    weight = []
    for s in range(NY):
        part = lax.dynamic_slice_in_dim(out_weight, ((y + s) % NY) * columns, columns, axis=1)
        weight.append(part if s == 0 else lax.ppermute(part, "head", shift(NY, s)))
    total = None
    for c in range(2):
        pieces = ahead[c] + behind[c][:0:-1]
        messages = attend(c, lists, all_queries, pieces, *far[c])
        shares = [messages[0]] + [
            lax.ppermute(messages[s], "x", shift(NX, -s)) for s in range(1, NX)
        ]
        att = join(shares)
        everyone = [att] + [lax.ppermute(att, "head", shift(NY, s)) for s in range(1, NY)]
        total = project(c, everyone, weight, total)
    return total


def solution(mesh):
    devices = mesh.devices.reshape(mesh.devices.shape[0], NZ, NX, NY)
    grid = Mesh(devices, ("batch", "z", "x", "head"))
    rows = ("batch", "z", "x")
    in_specs = (
        P(rows, "head"),
        P(rows, None, "head"),
        P("head", None),
        P("batch", None),
        P("batch"),
    )
    return jax.shard_map(
        body, mesh=grid, in_specs=in_specs, out_specs=P(rows, "head"), check_vma=False
    )
```

```python
import functools
import math

import jax
import jax.numpy as jnp
from jax import lax
from jax.experimental import pallas as pl
from jax.experimental.pallas import tpu as pltpu
from jax.sharding import Mesh
from jax.sharding import PartitionSpec as P

DH = 128
BLK = 64
NEG = -1e30
NZ = 8
NX = 4
NY = 4
BPD = 8
TOK = BLK * BPD
HEADS = 4
ALL = HEADS * DH
PAIR = 2
WIDE = PAIR * DH
STAT = 16
GROUP = 4
QBS = NX * BPD
COUNT, LISTED, ORDER = QBS, QBS * 8 + 8, QBS + 8
INDEX_AT = 2 * COUNT
ORDER_AT = INDEX_AT + 2 * LISTED
DENSE_AT = ORDER_AT + 2 * ORDER
X_AT = DENSE_AT + 2
PLAN = X_AT + 1
STAGES = ((0, 1, 2, 6, 7), (3, 4, 5))
SLOTS = [stage * 8 + part.index(p) for p in range(8) for stage, part in enumerate(STAGES) if p in part]
COUNT, LISTED, ORDER = QBS, QBS * 8 + 8, QBS + 8
INDEX_AT = len(STAGES) * COUNT
ORDER_AT = INDEX_AT + len(STAGES) * LISTED
DENSE_AT = ORDER_AT + len(STAGES) * ORDER
X_AT = DENSE_AT + 2
PLAN = X_AT + 1
SCALE = 1.0 / math.sqrt(DH)
SCALE2 = SCALE / math.log(2.0)
VMEM = 28 * 1024 * 1024

any_space = pl.BlockSpec(memory_space=pl.ANY)
in_vmem = pl.BlockSpec(memory_space=pltpu.VMEM)
in_smem = pl.BlockSpec(memory_space=pltpu.SMEM)


def shift(count, by):
    return [(i, (i + by) % count) for i in range(count)]


def plan_kernel(table, glob, place, slots, plan):
    z, x = place[0], place[1]
    plan[X_AT] = x
    for g in range(2):
        owner = glob[g] >> 3
        slot = (x - (owner & 3)) & 3
        plan[DENSE_AT + g] = jnp.where((owner >> 2) == z, slot * BPD + (glob[g] & 7), -1)

    def one(qb, carry):
        qx = (x - (qb >> 3)) & 3
        block = ((z * NX + qx) << 3) + (qb & 7)
        entries = [(block - 1, block > 0), (block, None)]
        entries += [(block + 1, block < NZ * NX * BPD - 1)]
        entries += [(glob[0], None), (glob[1], None)]
        entries += [(table[block * 3 + j], None) for j in range(3)]
        for stage in range(len(STAGES)):
            plan[stage * COUNT + qb] = 0
            for k in range(8):
                plan[INDEX_AT + stage * LISTED + qb * 8 + k] = 0
        for key, exists in entries:
            key = jnp.clip(key, 0, NZ * NX * BPD - 1)
            owner = key >> 3
            here = (owner & 3) == x
            if exists is not None:
                here = here & exists
            slot = slots[((owner >> 2) - z) & 7]
            stage, slot = slot >> 3, slot & 7
            filled = plan[stage * COUNT + qb]
            plan[INDEX_AT + stage * LISTED + qb * 8 + filled] = (slot << 3) + (key & 7)
            plan[stage * COUNT + qb] = filled + here.astype(jnp.int32)
        is_global = (block == glob[0]) | (block == glob[1])
        for stage in range(len(STAGES)):
            plan[stage * COUNT + qb] = jnp.where(is_global, 0, plan[stage * COUNT + qb])
        return carry

    lax.fori_loop(0, QBS, one, 0)

    def place_one(stage, pairs, qb, filled):
        plan[filled] = qb
        return filled + (((plan[stage * COUNT + qb] + 1) >> 1) == pairs).astype(jnp.int32)

    for stage in range(len(STAGES)):
        filled = jnp.int32(ORDER_AT + stage * ORDER)
        for pairs in range(4, -1, -1):
            filled = lax.fori_loop(0, QBS, functools.partial(place_one, stage, pairs), filled)


def make_plan(table, glob, place):
    return pl.pallas_call(
        plan_kernel,
        out_shape=jax.ShapeDtypeStruct((PLAN,), jnp.int32),
        in_specs=[in_smem] * 4,
        out_specs=in_smem,
        compiler_params=pltpu.CompilerParams(vmem_limit_bytes=1024 * 1024),
    )(table, glob, place, jnp.array(SLOTS, jnp.int32))


def dot_t(a, b):
    return lax.dot_general(a, b, (((1,), (1,)), ((), ())), preferred_element_type=jnp.float32)


def attend_kernel(stage, *refs):
    plan, q_in, own_q = refs[:3]
    o_s, stat, q_s, kv_s, wide, sems = refs[-6:]
    slots = kv_s.shape[0]
    copies = [(own_q, q_s.at[0])]
    copies += [(q_in.at[(plan[X_AT] - s) & 3], q_s.at[s]) for s in range(1, NX)]
    out, at_ref = [], 3
    for slot, piece in enumerate(STAGES[stage]):
        if piece == NZ // 2:
            copies += [(refs[at_ref + k], kv_s.at[slot, k]) for k in range(2)]
        else:
            copies.append((refs[at_ref], kv_s.at[slot]))
        at_ref += 2 if piece == NZ // 2 else 1
    if stage > 0:
        copies += [(refs[at_ref], o_s), (refs[at_ref + 1], stat)]
        at_ref += 2
    last = stage == len(STAGES) - 1
    if last:
        for c in range(HEADS // PAIR):
            for s in range(NX):
                part = o_s.at[s, :, pl.ds(c * WIDE, WIDE)]
                out.append((part, refs[at_ref + c * NX + s]))
    else:
        out = [(o_s, refs[at_ref]), (stat, refs[at_ref + 1])]
    copies = [pltpu.make_async_copy(a, b, sems.at[n]) for n, (a, b) in enumerate(copies)]
    for copy in copies:
        copy.start()
    for copy in copies:
        copy.wait()

    def share(top, both):
        total = both[:, DH:]
        return both[:, :DH] / total, top * SCALE + jnp.log(total)

    def at(qb, head):
        rows = pl.ds(pl.multiple_of((qb & 7) * BLK, BLK), BLK)
        return (qb >> 3, rows, slice(head * DH, (head + 1) * DH)), (
            head,
            pl.ds(pl.multiple_of(qb * BLK, BLK), BLK),
            slice(None),
        )

    def merge(qb, head, part, lse):
        if stage == 0:
            return part.astype(jnp.bfloat16), lse
        here, line = at(qb, head)
        before = stat[line]
        top = jnp.maximum(before, lse)
        old, new = jnp.exp(before - top), jnp.exp(lse - top)
        both = old + new
        part = (o_s[here].astype(jnp.float32) * old + part * new) / both
        return part.astype(jnp.bfloat16), top + jnp.log(both)

    def finish(qb, head, part, lse):
        here, line = at(qb, head)
        o_s[here] = part
        stat[line] = lse

    def load_q(qb, head):
        rows = pl.ds(pl.multiple_of((qb & 7) * BLK, BLK), BLK)
        return q_s[qb >> 3, rows, head * DH : (head + 1) * DH]

    lane = lax.broadcasted_iota(jnp.int32, (BLK, 2 * BLK), 1)

    def group(g, pairs):
        blocks = [plan[ORDER_AT + stage * ORDER + g * GROUP + i] for i in range(GROUP)]
        counts = [plan[stage * COUNT + qb] for qb in blocks]
        where = []
        for i in range(GROUP):
            first = INDEX_AT + stage * LISTED + blocks[i] * 8
            entries = [plan[first + e] for e in range(2 * pairs)]
            where.append(
                [(e >> 3, pl.ds(pl.multiple_of((e & 7) * BLK, BLK), BLK)) for e in entries]
            )

        def load(i, h, t, kind):
            cols = slice(h * DH, (h + 1) * DH)
            both = [kv_s[piece, kind, rows, cols] for piece, rows in where[i][2 * t : 2 * t + 2]]
            return jnp.concatenate(both, axis=0)

        chains = [(i, h) for i in range(GROUP) for h in range(HEADS)]
        queries = [load_q(blocks[i], h) for i, h in chains]
        scores = [
            [
                jnp.where(
                    lane < (counts[i] - 2 * t) * BLK, dot_t(query, load(i, h, t, 0)), NEG
                )
                for t in range(pairs)
            ]
            for query, (i, h) in zip(queries, chains)
        ]
        tops = [
            jnp.max(functools.reduce(jnp.maximum, tiles), axis=1, keepdims=True)
            for tiles in scores
        ]
        weights = [
            [jnp.exp2((tile - top) * SCALE2).astype(jnp.bfloat16) for tile in tiles]
            for tiles, top in zip(scores, tops)
        ]
        sums = []
        for (i, h), tiles in zip(chains, weights):
            both = None
            for t in range(pairs):
                values = load(i, h, t, 1)
                values = jnp.concatenate([values, jnp.ones_like(values)], axis=1)
                term = jnp.dot(tiles[t], values, preferred_element_type=jnp.float32)
                both = term if both is None else both + term
            sums.append(both)
        shares = [share(top, both) for top, both in zip(tops, sums)]
        merged = [
            merge(blocks[i], h, part, jnp.where(counts[i] > 0, lse, NEG))
            for (i, h), (part, lse) in zip(chains, shares)
        ]
        for (i, h), (part, lse) in zip(chains, merged):
            finish(blocks[i], h, part, lse)

    def nothing(g):
        for i in range(GROUP):
            qb = plan[ORDER_AT + stage * ORDER + g * GROUP + i]
            for h in range(HEADS):
                finish(
                    qb, h, jnp.zeros((BLK, DH), jnp.bfloat16), jnp.full((BLK, DH), NEG, jnp.float32)
                )

    def any_group(g, carry):
        most = (plan[stage * COUNT + plan[ORDER_AT + stage * ORDER + g * GROUP]] + 1) >> 1
        if stage == 0:
            pl.when(most == 0)(functools.partial(nothing, g))
        for pairs in range(1, 5):
            pl.when(most == pairs)(functools.partial(group, g, pairs))
        return carry

    lax.fori_loop(0, QBS // GROUP, any_group, 0)

    for g in range(2):

        @pl.when(plan[DENSE_AT + g] >= 0)
        def _(g=g):
            qb = plan[DENSE_AT + g]
            queries = [load_q(qb, h) for h in range(HEADS)]

            def score(p, tops):
                tiles = [
                    dot_t(queries[h], kv_s[p, 0, :, h * DH : (h + 1) * DH]) for h in range(HEADS)
                ]
                for h in range(HEADS):
                    wide[h, p] = tiles[h]
                parts = [
                    [tile[:, t * DH : (t + 1) * DH] for t in range(TOK // DH)] for tile in tiles
                ]
                return tuple(
                    functools.reduce(jnp.maximum, part, top) for part, top in zip(parts, tops)
                )

            low = jnp.full((BLK, DH), NEG, jnp.float32)
            tops = lax.fori_loop(0, slots, score, (low,) * HEADS)
            tops = [jnp.max(top, axis=1, keepdims=True) for top in tops]

            def gather(p, sums):
                done = []
                for h in range(HEADS):
                    weights = jnp.exp2((wide[h, p] - tops[h]) * SCALE2).astype(jnp.bfloat16)
                    values = kv_s[p, 1, :, h * DH : (h + 1) * DH]
                    values = jnp.concatenate([values, jnp.ones_like(values)], axis=1)
                    done.append(
                        sums[h] + jnp.dot(weights, values, preferred_element_type=jnp.float32)
                    )
                return tuple(done)

            none = jnp.zeros((BLK, 2 * DH), jnp.float32)
            sums = lax.fori_loop(0, slots, gather, (none,) * HEADS)
            for h in range(HEADS):
                finish(qb, h, *merge(qb, h, *share(tops[h], sums[h])))

    eye = lax.broadcasted_iota(jnp.int32, (DH, DH), 0) == lax.broadcasted_iota(
        jnp.int32, (DH, DH), 1
    )
    for s in range(NX if last else 0):
        for h in range(HEADS):
            lines = []
            for t in range(TOK // DH):
                tile = stat[h, s * TOK + t * DH : s * TOK + (t + 1) * DH, :]
                lines.append(jnp.sum(jnp.where(eye, tile, 0.0), axis=0, keepdims=True))
            left = jnp.concatenate(lines, axis=0)
            terms = []
            for _ in range(3):
                term = left.astype(jnp.bfloat16).astype(jnp.float32)
                terms.append(term)
                left = left - term
            terms.append(jnp.zeros_like(left))
            o_s[s, TOK : TOK + STAT, h * DH : (h + 1) * DH] = jnp.concatenate(
                terms, axis=0
            ).astype(jnp.bfloat16)
    back = [pltpu.make_async_copy(a, b, sems.at[n]) for n, (a, b) in enumerate(out)]
    for copy in back:
        copy.start()
    for copy in back:
        copy.wait()


def attend(stage, plan, queries, pieces, before=()):
    slots = len(STAGES[stage])
    arrays = [*queries, *pieces, *before]
    rows = TOK + STAT
    held = [
        jax.ShapeDtypeStruct((NX, rows, ALL), jnp.bfloat16),
        jax.ShapeDtypeStruct((HEADS, NX * TOK, DH), jnp.float32),
    ]
    message = jax.ShapeDtypeStruct((rows, WIDE), jnp.bfloat16)
    last = stage == len(STAGES) - 1
    out_shape = [message] * (NX * HEADS // PAIR) if last else held
    return pl.pallas_call(
        functools.partial(attend_kernel, stage),
        out_shape=out_shape,
        in_specs=[in_smem] + [any_space] * len(arrays),
        out_specs=[any_space] * len(out_shape),
        scratch_shapes=[
            pltpu.VMEM((NX, rows, ALL), jnp.bfloat16),
            pltpu.VMEM((HEADS, NX * TOK, DH), jnp.float32),
            pltpu.VMEM((NX, TOK, ALL), jnp.bfloat16),
            pltpu.VMEM((slots, 2, TOK, ALL), jnp.bfloat16),
            pltpu.VMEM((HEADS, slots, BLK, TOK), jnp.float32),
            pltpu.SemaphoreType.DMA((24,)),
        ],
        compiler_params=pltpu.CompilerParams(vmem_limit_bytes=VMEM),
        cost_estimate=pl.CostEstimate(
            flops=8_000_000_000, bytes_accessed=24_000_000, transcendentals=4_000_000
        ),
    )(plan, *arrays)


def join_kernel(*refs):
    shares, out = refs[:-1], refs[-1]
    eye = lax.broadcasted_iota(jnp.int32, (DH, DH), 0) == lax.broadcasted_iota(
        jnp.int32, (DH, DH), 1
    )
    for h in range(PAIR):
        cols = slice(h * DH, (h + 1) * DH)
        stats = []
        for share in shares:
            terms = share[TOK : TOK + STAT, cols].astype(jnp.float32)
            stats.append(terms[0:4] + terms[4:8] + terms[8:12])
        for t in range(TOK // DH):
            lse = [
                jnp.sum(
                    jnp.where(eye, jnp.broadcast_to(s[t : t + 1], (DH, DH)), 0.0),
                    axis=1,
                    keepdims=True,
                )
                for s in stats
            ]
            top = functools.reduce(jnp.maximum, lse)
            scale = [jnp.exp(v - top) for v in lse]
            norm = functools.reduce(jnp.add, scale)
            rows = slice(t * DH, (t + 1) * DH)
            terms = [f * s[rows, cols].astype(jnp.float32) for f, s in zip(scale, shares)]
            out[rows, cols] = (functools.reduce(jnp.add, terms) / norm).astype(jnp.bfloat16)


def join(messages):
    return pl.pallas_call(
        join_kernel,
        out_shape=jax.ShapeDtypeStruct((TOK, WIDE), jnp.bfloat16),
        in_specs=[in_vmem] * len(messages),
        out_specs=in_vmem,
        compiler_params=pltpu.CompilerParams(vmem_limit_bytes=VMEM),
        cost_estimate=pl.CostEstimate(
            flops=4_000_000, bytes_accessed=1_300_000, transcendentals=8_000
        ),
    )(*messages)


def project_kernel(last, *refs):
    att, weight = refs[:NY], refs[NY : 2 * NY]
    total = functools.reduce(
        jnp.add,
        [jnp.dot(a[...], w[...], preferred_element_type=jnp.float32) for a, w in zip(att, weight)],
    )
    if last:
        total = total + refs[2 * NY][...]
    refs[-1][...] = total.astype(refs[-1].dtype)


def project(chunk, att, weight, so_far=None):
    last = so_far is not None
    columns = weight[0].shape[1]
    tile = 256
    out_spec = pl.BlockSpec((TOK, tile), lambda j: (0, j))
    return pl.pallas_call(
        functools.partial(project_kernel, last),
        grid=(columns // tile,),
        out_shape=jax.ShapeDtypeStruct((TOK, columns), jnp.bfloat16 if last else jnp.float32),
        in_specs=[pl.BlockSpec((TOK, WIDE), lambda j: (0, 0))] * NY
        + [pl.BlockSpec((WIDE, tile), lambda j: (chunk, j))] * NY
        + [out_spec] * last,
        out_specs=out_spec,
        compiler_params=pltpu.CompilerParams(vmem_limit_bytes=VMEM),
        cost_estimate=pl.CostEstimate(
            flops=1_073_741_824, bytes_accessed=5_000_000, transcendentals=0
        ),
    )(*att, *weight, *([so_far] if last else []))


def ring_step(right, left):
    return (
        lax.ppermute(right, "z", shift(NZ, 1)),
        lax.ppermute(left, "z", shift(NZ, -1)),
    )


def after(value, *others):
    return lax.optimization_barrier((value, others))[0]


def body(queries, key_value, out_weight, random_blocks, global_ids):
    z, x, y = lax.axis_index("z"), lax.axis_index("x"), lax.axis_index("head")
    own = jnp.transpose(key_value, (1, 0, 2))
    place = jnp.stack([z, x]).astype(jnp.int32)
    plane = (lax.all_gather(queries, "x"), queries)
    first = ring_step(own, own)
    plan = make_plan(random_blocks.reshape(-1), global_ids, place)
    columns = out_weight.shape[1] // NY
    weight = [
        lax.dynamic_slice_in_dim(out_weight, ((y + s) % NY) * columns, columns, axis=1)
        for s in range(NY)
    ]
    w1, w3 = (lax.ppermute(weight[s], "head", shift(NY, s)) for s in (1, 3))
    second = ring_step(*after(first, plan, weight))
    w2 = lax.ppermute(after(weight[2], w1, w3), "head", shift(NY, 2))
    third = ring_step(*after(second, w1, w3))
    near = [own, first[1], second[1], second[0], first[0]]
    held = attend(0, plan, plane, near)
    third = after(third, held, w2)
    fourth = ring_step(third[0][0], third[1][1])
    messages = attend(1, plan, plane, [third[1], *fourth, third[0]], held)
    weight = [weight[0], w1, w2, w3]
    total = None
    for c in range(HEADS // PAIR):
        sent = messages[c * NX : (c + 1) * NX]
        shares = [sent[0]] + [lax.ppermute(sent[s], "x", shift(NX, -s)) for s in range(1, NX)]
        att = join(shares)
        everyone = [att] + [lax.ppermute(att, "head", shift(NY, s)) for s in range(1, NY)]
        total = project(c, everyone, weight, total)
    return total


def solution(mesh):
    devices = mesh.devices.reshape(mesh.devices.shape[0], NZ, NX, NY)
    grid = Mesh(devices, ("batch", "z", "x", "head"))
    rows = ("batch", "z", "x")
    in_specs = (
        P(rows, "head"),
        P(rows, None, "head"),
        P("head", None),
        P("batch", None),
        P("batch"),
    )
    return jax.shard_map(
        body, mesh=grid, in_specs=in_specs, out_specs=P(rows, "head"), check_vma=False
    )
```

```python
import functools
import math

import jax
import jax.numpy as jnp
from jax import lax
from jax.experimental import pallas as pl
from jax.experimental.pallas import tpu as pltpu
from jax.sharding import Mesh
from jax.sharding import PartitionSpec as P

DH = 128
BLK = 64
NEG = -1e30
NZ = 8
NX = 4
NY = 4
BPD = 8
TOK = BLK * BPD
HEADS = 4
ALL = HEADS * DH
PAIR = 2
WIDE = PAIR * DH
STAT = 16
CHAINS = 16
QBS = NX * BPD
COUNT, LISTED, ORDER = QBS, QBS * 8 + 8, QBS + 8
INDEX_AT = 2 * COUNT
ORDER_AT = INDEX_AT + 2 * LISTED
DENSE_AT = ORDER_AT + 2 * ORDER
X_AT = DENSE_AT + 2
PLAN = X_AT + 1
STAGES = ((0, 1, 2, 6, 7), (3, 5), (4,))
SLOTS = [stage * 8 + part.index(p) for p in range(8) for stage, part in enumerate(STAGES) if p in part]
COUNT, LISTED, ORDER = QBS, QBS * 8 + 8, QBS + 8
INDEX_AT = len(STAGES) * COUNT
ORDER_AT = INDEX_AT + len(STAGES) * LISTED
DENSE_AT = ORDER_AT + len(STAGES) * ORDER
X_AT = DENSE_AT + 2
PLAN = X_AT + 1
SCALE = 1.0 / math.sqrt(DH)
SCALE2 = SCALE / math.log(2.0)
VMEM = 20 * 1024 * 1024

any_space = pl.BlockSpec(memory_space=pl.ANY)
in_vmem = pl.BlockSpec(memory_space=pltpu.VMEM)
in_smem = pl.BlockSpec(memory_space=pltpu.SMEM)


def shift(count, by):
    return [(i, (i + by) % count) for i in range(count)]


def plan_kernel(table, glob, place, slots, plan):
    z, x = place[0], place[1]
    plan[X_AT] = x
    for g in range(2):
        owner = glob[g] >> 3
        slot = (x - (owner & 3)) & 3
        plan[DENSE_AT + g] = jnp.where((owner >> 2) == z, slot * BPD + (glob[g] & 7), -1)

    def one(qb, carry):
        qx = (x - (qb >> 3)) & 3
        block = ((z * NX + qx) << 3) + (qb & 7)
        entries = [(block - 1, block > 0), (block, None)]
        entries += [(block + 1, block < NZ * NX * BPD - 1)]
        entries += [(glob[0], None), (glob[1], None)]
        entries += [(table[block * 3 + j], None) for j in range(3)]
        for stage in range(len(STAGES)):
            plan[stage * COUNT + qb] = 0
            for k in range(8):
                plan[INDEX_AT + stage * LISTED + qb * 8 + k] = 0
        for key, exists in entries:
            key = jnp.clip(key, 0, NZ * NX * BPD - 1)
            owner = key >> 3
            here = (owner & 3) == x
            if exists is not None:
                here = here & exists
            slot = slots[((owner >> 2) - z) & 7]
            stage, slot = slot >> 3, slot & 7
            filled = plan[stage * COUNT + qb]
            plan[INDEX_AT + stage * LISTED + qb * 8 + filled] = (slot << 3) + (key & 7)
            plan[stage * COUNT + qb] = filled + here.astype(jnp.int32)
        is_global = (block == glob[0]) | (block == glob[1])
        for stage in range(len(STAGES)):
            plan[stage * COUNT + qb] = jnp.where(is_global, 0, plan[stage * COUNT + qb])
        return carry

    lax.fori_loop(0, QBS, one, 0)

    def place_one(stage, pairs, qb, filled):
        plan[filled] = qb
        return filled + (((plan[stage * COUNT + qb] + 1) >> 1) == pairs).astype(jnp.int32)

    for stage in range(len(STAGES)):
        filled = jnp.int32(ORDER_AT + stage * ORDER)
        for pairs in range(4, -1, -1):
            filled = lax.fori_loop(0, QBS, functools.partial(place_one, stage, pairs), filled)


def make_plan(table, glob, place):
    return pl.pallas_call(
        plan_kernel,
        out_shape=jax.ShapeDtypeStruct((PLAN,), jnp.int32),
        in_specs=[in_smem] * 4,
        out_specs=in_smem,
        compiler_params=pltpu.CompilerParams(vmem_limit_bytes=1024 * 1024),
    )(table, glob, place, jnp.array(SLOTS, jnp.int32))


def dot_t(a, b):
    return lax.dot_general(a, b, (((1,), (1,)), ((), ())), preferred_element_type=jnp.float32)


def attend_kernel(stage, heads, *refs):
    plan = refs[0]
    at_once = CHAINS // len(heads)
    kv_s, wide, sems = refs[-3:]
    slots = kv_s.shape[0]
    last = stage == len(STAGES) - 1
    if stage == 0:
        q_s, o_s, stat = refs[-6:-3]
        copies = [(refs[1 + s], q_s.at[s]) for s in range(NX)]
        at_ref = 1 + NX
    else:
        q_s = refs[1]
        copies, at_ref = [], 4
        outs = refs[-9:-3] if last else refs[-5:-3]
        o_s, stat = outs[:2]
    for slot, piece in enumerate(STAGES[stage]):
        if piece == NZ // 2:
            copies += [(refs[at_ref + k], kv_s.at[slot, k]) for k in range(2)]
        else:
            copies.append((refs[at_ref], kv_s.at[slot]))
        at_ref += 1
    cols = pl.ds(heads[0] * DH, len(heads) * DH)
    out = [(o_s.at[s, :, cols], outs[2 + s]) for s in range(NX)] if last else []
    copies = [pltpu.make_async_copy(a, b, sems.at[n]) for n, (a, b) in enumerate(copies)]
    for copy in copies:
        copy.start()
    for copy in copies:
        copy.wait()

    def share(top, both):
        total = both[:, DH:]
        return both[:, :DH] / total, top * SCALE + jnp.log(total)

    def at(qb, head):
        rows = pl.ds(pl.multiple_of((qb & 7) * BLK, BLK), BLK)
        return (qb >> 3, rows, slice(head * DH, (head + 1) * DH)), (
            head,
            pl.ds(pl.multiple_of(qb * BLK, BLK), BLK),
            slice(None),
        )

    def merge(qb, head, part, lse):
        if stage == 0:
            return part.astype(jnp.bfloat16), lse
        here, line = at(qb, head)
        before = stat[line]
        top = jnp.maximum(before, lse)
        old, new = jnp.exp(before - top), jnp.exp(lse - top)
        both = old + new
        part = (o_s[here].astype(jnp.float32) * old + part * new) / both
        return part.astype(jnp.bfloat16), top + jnp.log(both)

    def finish(qb, head, part, lse):
        here, line = at(qb, head)
        o_s[here] = part
        stat[line] = lse

    def load_q(qb, head):
        rows = pl.ds(pl.multiple_of((qb & 7) * BLK, BLK), BLK)
        return q_s[qb >> 3, rows, head * DH : (head + 1) * DH]

    lane = lax.broadcasted_iota(jnp.int32, (BLK, 2 * BLK), 1)

    def group(g, pairs):
        blocks = [plan[ORDER_AT + stage * ORDER + g * at_once + i] for i in range(at_once)]
        counts = [plan[stage * COUNT + qb] for qb in blocks]
        where = []
        for i in range(at_once):
            first = INDEX_AT + stage * LISTED + blocks[i] * 8
            entries = [plan[first + e] for e in range(2 * pairs)]
            where.append(
                [(e >> 3, pl.ds(pl.multiple_of((e & 7) * BLK, BLK), BLK)) for e in entries]
            )

        def load(i, h, t, kind):
            cols = slice(h * DH, (h + 1) * DH)
            both = [kv_s[piece, kind, rows, cols] for piece, rows in where[i][2 * t : 2 * t + 2]]
            return jnp.concatenate(both, axis=0)

        chains = [(i, h) for i in range(at_once) for h in heads]
        queries = [load_q(blocks[i], h) for i, h in chains]
        scores = [
            [
                jnp.where(
                    lane < (counts[i] - 2 * t) * BLK, dot_t(query, load(i, h, t, 0)), NEG
                )
                for t in range(pairs)
            ]
            for query, (i, h) in zip(queries, chains)
        ]
        tops = [
            jnp.max(functools.reduce(jnp.maximum, tiles), axis=1, keepdims=True)
            for tiles in scores
        ]
        weights = [
            [jnp.exp2((tile - top) * SCALE2).astype(jnp.bfloat16) for tile in tiles]
            for tiles, top in zip(scores, tops)
        ]
        sums = []
        for (i, h), tiles in zip(chains, weights):
            both = None
            for t in range(pairs):
                values = load(i, h, t, 1)
                values = jnp.concatenate([values, jnp.ones_like(values)], axis=1)
                term = jnp.dot(tiles[t], values, preferred_element_type=jnp.float32)
                both = term if both is None else both + term
            sums.append(both)
        shares = [share(top, both) for top, both in zip(tops, sums)]
        merged = [
            merge(blocks[i], h, part, jnp.where(counts[i] > 0, lse, NEG))
            for (i, h), (part, lse) in zip(chains, shares)
        ]
        for (i, h), (part, lse) in zip(chains, merged):
            finish(blocks[i], h, part, lse)

    def nothing(g):
        for i in range(at_once):
            qb = plan[ORDER_AT + stage * ORDER + g * at_once + i]
            for h in heads:
                finish(
                    qb, h, jnp.zeros((BLK, DH), jnp.bfloat16), jnp.full((BLK, DH), NEG, jnp.float32)
                )

    def any_group(g, carry):
        most = (plan[stage * COUNT + plan[ORDER_AT + stage * ORDER + g * at_once]] + 1) >> 1
        if stage == 0:
            pl.when(most == 0)(functools.partial(nothing, g))
        for pairs in range(1, 5):
            pl.when(most == pairs)(functools.partial(group, g, pairs))
        return carry

    lax.fori_loop(0, QBS // at_once, any_group, 0)

    for g in range(2):

        @pl.when(plan[DENSE_AT + g] >= 0)
        def _(g=g):
            qb = plan[DENSE_AT + g]
            queries = [load_q(qb, h) for h in heads]

            def score(p, tops):
                tiles = [
                    dot_t(query, kv_s[p, 0, :, h * DH : (h + 1) * DH])
                    for query, h in zip(queries, heads)
                ]
                for n, tile in enumerate(tiles):
                    wide[n, p] = tile
                parts = [
                    [tile[:, t * DH : (t + 1) * DH] for t in range(TOK // DH)] for tile in tiles
                ]
                return tuple(
                    functools.reduce(jnp.maximum, part, top) for part, top in zip(parts, tops)
                )

            low = jnp.full((BLK, DH), NEG, jnp.float32)
            tops = lax.fori_loop(0, slots, score, (low,) * len(heads))
            tops = [jnp.max(top, axis=1, keepdims=True) for top in tops]

            def gather(p, sums):
                done = []
                for n, h in enumerate(heads):
                    weights = jnp.exp2((wide[n, p] - tops[n]) * SCALE2).astype(jnp.bfloat16)
                    values = kv_s[p, 1, :, h * DH : (h + 1) * DH]
                    values = jnp.concatenate([values, jnp.ones_like(values)], axis=1)
                    done.append(
                        sums[n] + jnp.dot(weights, values, preferred_element_type=jnp.float32)
                    )
                return tuple(done)

            none = jnp.zeros((BLK, 2 * DH), jnp.float32)
            sums = lax.fori_loop(0, slots, gather, (none,) * len(heads))
            for n, h in enumerate(heads):
                finish(qb, h, *merge(qb, h, *share(tops[n], sums[n])))

    eye = lax.broadcasted_iota(jnp.int32, (DH, DH), 0) == lax.broadcasted_iota(
        jnp.int32, (DH, DH), 1
    )
    for s in range(NX if last else 0):
        for h in heads:
            lines = []
            for t in range(TOK // DH):
                tile = stat[h, s * TOK + t * DH : s * TOK + (t + 1) * DH, :]
                lines.append(jnp.sum(jnp.where(eye, tile, 0.0), axis=0, keepdims=True))
            left = jnp.concatenate(lines, axis=0)
            terms = []
            for _ in range(3):
                term = left.astype(jnp.bfloat16).astype(jnp.float32)
                terms.append(term)
                left = left - term
            terms.append(jnp.zeros_like(left))
            o_s[s, TOK : TOK + STAT, h * DH : (h + 1) * DH] = jnp.concatenate(
                terms, axis=0
            ).astype(jnp.bfloat16)
    back = [pltpu.make_async_copy(a, b, sems.at[n]) for n, (a, b) in enumerate(out)]
    for copy in back:
        copy.start()
    for copy in back:
        copy.wait()


def attend(stage, plan, queries, pieces, before=(), heads=tuple(range(HEADS))):
    slots = len(STAGES[stage])
    rows = TOK + STAT
    last = stage == len(STAGES) - 1
    held = [
        jax.ShapeDtypeStruct((NX, rows, ALL), jnp.bfloat16),
        jax.ShapeDtypeStruct((HEADS, NX * TOK, DH), jnp.float32),
    ]
    message = jax.ShapeDtypeStruct((rows, len(heads) * DH), jnp.bfloat16)
    if stage == 0:
        arrays = [*queries, *pieces]
        in_specs = [any_space] * len(arrays)
        out_shape = [jax.ShapeDtypeStruct((NX, TOK, ALL), jnp.bfloat16), *held]
        aliases = {}
    else:
        arrays = [queries, *before, *pieces]
        in_specs = [in_vmem] * 3 + [any_space] * len(pieces)
        out_shape = held + [message] * (NX if last else 0)
        aliases = {2: 0, 3: 1}
    return pl.pallas_call(
        functools.partial(attend_kernel, stage, heads),
        out_shape=out_shape,
        in_specs=[in_smem] + in_specs,
        out_specs=[in_vmem] * len(out_shape),
        input_output_aliases=aliases,
        scratch_shapes=[
            pltpu.VMEM((slots, 2, TOK, ALL), jnp.bfloat16),
            pltpu.VMEM((len(heads), slots, BLK, TOK), jnp.float32),
            pltpu.SemaphoreType.DMA((NX + 6,)),
        ],
        compiler_params=pltpu.CompilerParams(vmem_limit_bytes=VMEM),
        cost_estimate=pl.CostEstimate(
            flops=8_000_000_000, bytes_accessed=24_000_000, transcendentals=4_000_000
        ),
    )(plan, *arrays)


def join_kernel(*refs):
    shares, out = refs[:-1], refs[-1]
    eye = lax.broadcasted_iota(jnp.int32, (DH, DH), 0) == lax.broadcasted_iota(
        jnp.int32, (DH, DH), 1
    )
    for h in range(PAIR):
        cols = slice(h * DH, (h + 1) * DH)
        stats = []
        for share in shares:
            terms = share[TOK : TOK + STAT, cols].astype(jnp.float32)
            stats.append(terms[0:4] + terms[4:8] + terms[8:12])
        for t in range(TOK // DH):
            lse = [
                jnp.sum(
                    jnp.where(eye, jnp.broadcast_to(s[t : t + 1], (DH, DH)), 0.0),
                    axis=1,
                    keepdims=True,
                )
                for s in stats
            ]
            top = functools.reduce(jnp.maximum, lse)
            scale = [jnp.exp(v - top) for v in lse]
            norm = functools.reduce(jnp.add, scale)
            rows = slice(t * DH, (t + 1) * DH)
            terms = [f * s[rows, cols].astype(jnp.float32) for f, s in zip(scale, shares)]
            out[rows, cols] = (functools.reduce(jnp.add, terms) / norm).astype(jnp.bfloat16)


def join(messages):
    return pl.pallas_call(
        join_kernel,
        out_shape=jax.ShapeDtypeStruct((TOK, WIDE), jnp.bfloat16),
        in_specs=[in_vmem] * len(messages),
        out_specs=in_vmem,
        compiler_params=pltpu.CompilerParams(vmem_limit_bytes=VMEM),
        cost_estimate=pl.CostEstimate(
            flops=4_000_000, bytes_accessed=1_300_000, transcendentals=8_000
        ),
    )(*messages)


def project_kernel(*refs):
    att, weight, out = refs[: -NY - 1], refs[-NY - 1 : -1], refs[-1]
    terms = []
    for n, part in enumerate(att):
        c, s = divmod(n, NY)
        rows = weight[s][c * WIDE : (c + 1) * WIDE, :]
        terms.append(jnp.dot(part[...], rows, preferred_element_type=jnp.float32))
    out[...] = functools.reduce(jnp.add, terms).astype(out.dtype)


def project(att, weight):
    columns = weight[0].shape[1]
    tile = 512
    return pl.pallas_call(
        project_kernel,
        grid=(columns // tile,),
        out_shape=jax.ShapeDtypeStruct((TOK, columns), jnp.bfloat16),
        in_specs=[pl.BlockSpec((TOK, WIDE), lambda j: (0, 0))] * len(att)
        + [pl.BlockSpec((ALL, tile), lambda j: (0, j))] * NY,
        out_specs=pl.BlockSpec((TOK, tile), lambda j: (0, j)),
        compiler_params=pltpu.CompilerParams(vmem_limit_bytes=VMEM),
        cost_estimate=pl.CostEstimate(
            flops=2_147_483_648, bytes_accessed=7_000_000, transcendentals=0
        ),
    )(*att, *weight)


def ring_step(right, left):
    return (
        lax.ppermute(right, "z", shift(NZ, 1)),
        lax.ppermute(left, "z", shift(NZ, -1)),
    )


def after(value, *others):
    return lax.optimization_barrier((value, others))[0]


def body(queries, key_value, out_weight, random_blocks, global_ids):
    z, x, y = lax.axis_index("z"), lax.axis_index("x"), lax.axis_index("head")
    own = jnp.transpose(key_value, (1, 0, 2))
    place = jnp.stack([z, x]).astype(jnp.int32)
    first = ring_step(own, own)
    plane = [queries] + [lax.ppermute(queries, "x", shift(NX, s)) for s in range(1, NX)]
    plan = make_plan(random_blocks.reshape(-1), global_ids, place)
    columns = out_weight.shape[1] // NY
    weight = [
        lax.dynamic_slice_in_dim(out_weight, ((y + s) % NY) * columns, columns, axis=1)
        for s in range(NY)
    ]
    second = ring_step(*after(first, plan, weight))
    w1, w3 = (lax.ppermute(after(weight[s], plane), "head", shift(NY, s)) for s in (1, 3))
    third = ring_step(*after(second, plane))
    near = [own, first[1], second[1], second[0], first[0]]
    plane, *held = attend(0, plan, plane, near)
    third = after(third, held, w1, w3)
    w2 = lax.ppermute(after(weight[2], w1, w3), "head", shift(NY, 2))
    fourth = ring_step(third[0][0], third[1][1])
    held = attend(1, plan, plane, [third[1], third[0]], held)
    held = after(held, w2)
    everyone = []
    for c in range(HEADS // PAIR):
        heads = tuple(range(c * PAIR, (c + 1) * PAIR))
        *held, m0, m1, m2, m3 = attend(2, plan, plane, fourth, held, heads)
        back = [lax.ppermute(m, "x", shift(NX, -s)) for s, m in ((1, m1), (2, m2), (3, m3))]
        att = join([m0, *back])
        everyone += [att] + [lax.ppermute(att, "head", shift(NY, s)) for s in range(1, NY)]
    return project(everyone, [weight[0], w1, w2, w3])


def solution(mesh):
    devices = mesh.devices.reshape(mesh.devices.shape[0], NZ, NX, NY)
    grid = Mesh(devices, ("batch", "z", "x", "head"))
    rows = ("batch", "z", "x")
    in_specs = (
        P(rows, "head"),
        P(rows, None, "head"),
        P("head", None),
        P("batch", None),
        P("batch"),
    )
    return jax.shard_map(
        body, mesh=grid, in_specs=in_specs, out_specs=P(rows, "head"), check_vma=False
    )
```

```python
import functools
import math

import jax
import jax.numpy as jnp
from jax import lax
from jax.experimental import pallas as pl
from jax.experimental.pallas import tpu as pltpu
from jax.sharding import Mesh
from jax.sharding import PartitionSpec as P

DH = 128
BLK = 64
NEG = -1e30
NZ = 8
NX = 4
NY = 4
BPD = 8
TOK = BLK * BPD
HEADS = 4
ALL = HEADS * DH
PAIR = 2
WIDE = PAIR * DH
STAT = 16
CHAINS = 16
TILE = 256
QBS = NX * BPD
COUNT, LISTED, ORDER = QBS, QBS * 8 + 8, QBS + 8
INDEX_AT = 2 * COUNT
ORDER_AT = INDEX_AT + 2 * LISTED
DENSE_AT = ORDER_AT + 2 * ORDER
X_AT = DENSE_AT + 2
PLAN = X_AT + 1
STAGES = ((0, 1, 2, 6, 7), (3, 5), (4,))
SLOTS = [stage * 8 + part.index(p) for p in range(8) for stage, part in enumerate(STAGES) if p in part]
COUNT, LISTED, ORDER = QBS, QBS * 8 + 8, QBS + 8
INDEX_AT = len(STAGES) * COUNT
ORDER_AT = INDEX_AT + len(STAGES) * LISTED
DENSE_AT = ORDER_AT + len(STAGES) * ORDER
X_AT = DENSE_AT + 2
PLAN = X_AT + 1
SCALE = 1.0 / math.sqrt(DH)
SCALE2 = SCALE / math.log(2.0)
VMEM = 20 * 1024 * 1024

any_space = pl.BlockSpec(memory_space=pl.ANY)
in_vmem = pl.BlockSpec(memory_space=pltpu.VMEM)
in_smem = pl.BlockSpec(memory_space=pltpu.SMEM)


def shift(count, by):
    return [(i, (i + by) % count) for i in range(count)]


def plan_kernel(table, glob, place, slots, plan):
    z, x = place[0], place[1]
    plan[X_AT] = x
    for g in range(2):
        owner = glob[g] >> 3
        slot = (x - (owner & 3)) & 3
        plan[DENSE_AT + g] = jnp.where((owner >> 2) == z, slot * BPD + (glob[g] & 7), -1)

    def one(qb, carry):
        qx = (x - (qb >> 3)) & 3
        block = ((z * NX + qx) << 3) + (qb & 7)
        entries = [(block - 1, block > 0), (block, None)]
        entries += [(block + 1, block < NZ * NX * BPD - 1)]
        entries += [(glob[0], None), (glob[1], None)]
        entries += [(table[block * 3 + j], None) for j in range(3)]
        for stage in range(len(STAGES)):
            plan[stage * COUNT + qb] = 0
            for k in range(8):
                plan[INDEX_AT + stage * LISTED + qb * 8 + k] = 0
        for key, exists in entries:
            key = jnp.clip(key, 0, NZ * NX * BPD - 1)
            owner = key >> 3
            here = (owner & 3) == x
            if exists is not None:
                here = here & exists
            slot = slots[((owner >> 2) - z) & 7]
            stage, slot = slot >> 3, slot & 7
            filled = plan[stage * COUNT + qb]
            plan[INDEX_AT + stage * LISTED + qb * 8 + filled] = (slot << 3) + (key & 7)
            plan[stage * COUNT + qb] = filled + here.astype(jnp.int32)
        is_global = (block == glob[0]) | (block == glob[1])
        for stage in range(len(STAGES)):
            plan[stage * COUNT + qb] = jnp.where(is_global, 0, plan[stage * COUNT + qb])
        return carry

    lax.fori_loop(0, QBS, one, 0)

    def place_one(stage, pairs, qb, filled):
        plan[filled] = qb
        return filled + (((plan[stage * COUNT + qb] + 1) >> 1) == pairs).astype(jnp.int32)

    for stage in range(len(STAGES)):
        filled = jnp.int32(ORDER_AT + stage * ORDER)
        for pairs in range(4, -1, -1):
            filled = lax.fori_loop(0, QBS, functools.partial(place_one, stage, pairs), filled)


def make_plan(table, glob, place):
    return pl.pallas_call(
        plan_kernel,
        out_shape=jax.ShapeDtypeStruct((PLAN,), jnp.int32),
        in_specs=[in_smem] * 4,
        out_specs=in_smem,
        compiler_params=pltpu.CompilerParams(vmem_limit_bytes=1024 * 1024),
    )(table, glob, place, jnp.array(SLOTS, jnp.int32))


def dot_t(a, b):
    return lax.dot_general(a, b, (((1,), (1,)), ((), ())), preferred_element_type=jnp.float32)


def attend_kernel(stage, heads, *refs):
    plan = refs[0]
    at_once = CHAINS // len(heads)
    kv_s, wide, sems = refs[-3:]
    slots = kv_s.shape[0]
    last = stage == len(STAGES) - 1
    if stage == 0:
        q_s, o_s, stat = refs[-6:-3]
        copies = [(refs[1 + s], q_s.at[s]) for s in range(NX)]
        at_ref = 1 + NX
    else:
        q_s = refs[1]
        copies, at_ref = [], 4
        outs = refs[-9:-3] if last else refs[-5:-3]
        o_s, stat = outs[:2]
    for slot, piece in enumerate(STAGES[stage]):
        if piece == NZ // 2:
            copies += [(refs[at_ref + k], kv_s.at[slot, k]) for k in range(2)]
        else:
            copies.append((refs[at_ref], kv_s.at[slot]))
        at_ref += 1
    cols = pl.ds(heads[0] * DH, len(heads) * DH)
    out = [(o_s.at[s, :, cols], outs[2 + s]) for s in range(NX)] if last else []
    copies = [pltpu.make_async_copy(a, b, sems.at[n]) for n, (a, b) in enumerate(copies)]
    for copy in copies:
        copy.start()
    for copy in copies:
        copy.wait()

    def share(top, both):
        total = both[:, DH:]
        return both[:, :DH] / total, top * SCALE + jnp.log(total)

    def at(qb, head):
        rows = pl.ds(pl.multiple_of((qb & 7) * BLK, BLK), BLK)
        return (qb >> 3, rows, slice(head * DH, (head + 1) * DH)), (
            head,
            pl.ds(pl.multiple_of(qb * BLK, BLK), BLK),
            slice(None),
        )

    def merge(qb, head, part, lse):
        if stage == 0:
            return part.astype(jnp.bfloat16), lse
        here, line = at(qb, head)
        before = stat[line]
        top = jnp.maximum(before, lse)
        old, new = jnp.exp(before - top), jnp.exp(lse - top)
        both = old + new
        part = (o_s[here].astype(jnp.float32) * old + part * new) / both
        return part.astype(jnp.bfloat16), top + jnp.log(both)

    def finish(qb, head, part, lse):
        here, line = at(qb, head)
        o_s[here] = part
        stat[line] = lse

    def load_q(qb, head):
        rows = pl.ds(pl.multiple_of((qb & 7) * BLK, BLK), BLK)
        return q_s[qb >> 3, rows, head * DH : (head + 1) * DH]

    lane = lax.broadcasted_iota(jnp.int32, (BLK, 2 * BLK), 1)

    def group(g, pairs):
        blocks = [plan[ORDER_AT + stage * ORDER + g * at_once + i] for i in range(at_once)]
        counts = [plan[stage * COUNT + qb] for qb in blocks]
        where = []
        for i in range(at_once):
            first = INDEX_AT + stage * LISTED + blocks[i] * 8
            entries = [plan[first + e] for e in range(2 * pairs)]
            where.append(
                [(e >> 3, pl.ds(pl.multiple_of((e & 7) * BLK, BLK), BLK)) for e in entries]
            )

        def load(i, h, t, kind):
            cols = slice(h * DH, (h + 1) * DH)
            both = [kv_s[piece, kind, rows, cols] for piece, rows in where[i][2 * t : 2 * t + 2]]
            return jnp.concatenate(both, axis=0)

        chains = [(i, h) for i in range(at_once) for h in heads]
        queries = [load_q(blocks[i], h) for i, h in chains]
        scores = [
            [
                jnp.where(
                    lane < (counts[i] - 2 * t) * BLK, dot_t(query, load(i, h, t, 0)), NEG
                )
                for t in range(pairs)
            ]
            for query, (i, h) in zip(queries, chains)
        ]
        tops = [
            jnp.max(functools.reduce(jnp.maximum, tiles), axis=1, keepdims=True)
            for tiles in scores
        ]
        weights = [
            [jnp.exp2((tile - top) * SCALE2).astype(jnp.bfloat16) for tile in tiles]
            for tiles, top in zip(scores, tops)
        ]
        sums = []
        for (i, h), tiles in zip(chains, weights):
            both = None
            for t in range(pairs):
                values = load(i, h, t, 1)
                values = jnp.concatenate([values, jnp.ones_like(values)], axis=1)
                term = jnp.dot(tiles[t], values, preferred_element_type=jnp.float32)
                both = term if both is None else both + term
            sums.append(both)
        shares = [share(top, both) for top, both in zip(tops, sums)]
        merged = [
            merge(blocks[i], h, part, jnp.where(counts[i] > 0, lse, NEG))
            for (i, h), (part, lse) in zip(chains, shares)
        ]
        for (i, h), (part, lse) in zip(chains, merged):
            finish(blocks[i], h, part, lse)

    def nothing(g):
        for i in range(at_once):
            qb = plan[ORDER_AT + stage * ORDER + g * at_once + i]
            for h in heads:
                finish(
                    qb, h, jnp.zeros((BLK, DH), jnp.bfloat16), jnp.full((BLK, DH), NEG, jnp.float32)
                )

    def any_group(g, carry):
        most = (plan[stage * COUNT + plan[ORDER_AT + stage * ORDER + g * at_once]] + 1) >> 1
        if stage == 0:
            pl.when(most == 0)(functools.partial(nothing, g))
        for pairs in range(1, 5):
            pl.when(most == pairs)(functools.partial(group, g, pairs))
        return carry

    lax.fori_loop(0, QBS // at_once, any_group, 0)

    for g in range(2):

        @pl.when(plan[DENSE_AT + g] >= 0)
        def _(g=g):
            qb = plan[DENSE_AT + g]
            queries = [load_q(qb, h) for h in heads]

            def score(p, tops):
                tiles = [
                    dot_t(query, kv_s[p, 0, :, h * DH : (h + 1) * DH])
                    for query, h in zip(queries, heads)
                ]
                for n, tile in enumerate(tiles):
                    wide[n, p] = tile
                parts = [
                    [tile[:, t * DH : (t + 1) * DH] for t in range(TOK // DH)] for tile in tiles
                ]
                return tuple(
                    functools.reduce(jnp.maximum, part, top) for part, top in zip(parts, tops)
                )

            low = jnp.full((BLK, DH), NEG, jnp.float32)
            tops = lax.fori_loop(0, slots, score, (low,) * len(heads))
            tops = [jnp.max(top, axis=1, keepdims=True) for top in tops]

            def gather(p, sums):
                done = []
                for n, h in enumerate(heads):
                    weights = jnp.exp2((wide[n, p] - tops[n]) * SCALE2).astype(jnp.bfloat16)
                    values = kv_s[p, 1, :, h * DH : (h + 1) * DH]
                    values = jnp.concatenate([values, jnp.ones_like(values)], axis=1)
                    done.append(
                        sums[n] + jnp.dot(weights, values, preferred_element_type=jnp.float32)
                    )
                return tuple(done)

            none = jnp.zeros((BLK, 2 * DH), jnp.float32)
            sums = lax.fori_loop(0, slots, gather, (none,) * len(heads))
            for n, h in enumerate(heads):
                finish(qb, h, *merge(qb, h, *share(tops[n], sums[n])))

    eye = lax.broadcasted_iota(jnp.int32, (DH, DH), 0) == lax.broadcasted_iota(
        jnp.int32, (DH, DH), 1
    )
    for s in range(NX if last else 0):
        for h in heads:
            lines = []
            for t in range(TOK // DH):
                tile = stat[h, s * TOK + t * DH : s * TOK + (t + 1) * DH, :]
                lines.append(jnp.sum(jnp.where(eye, tile, 0.0), axis=0, keepdims=True))
            left = jnp.concatenate(lines, axis=0)
            terms = []
            for _ in range(3):
                term = left.astype(jnp.bfloat16).astype(jnp.float32)
                terms.append(term)
                left = left - term
            terms.append(jnp.zeros_like(left))
            o_s[s, TOK : TOK + STAT, h * DH : (h + 1) * DH] = jnp.concatenate(
                terms, axis=0
            ).astype(jnp.bfloat16)
    back = [pltpu.make_async_copy(a, b, sems.at[n]) for n, (a, b) in enumerate(out)]
    for copy in back:
        copy.start()
    for copy in back:
        copy.wait()


def attend(stage, plan, queries, pieces, before=(), heads=tuple(range(HEADS))):
    slots = len(STAGES[stage])
    rows = TOK + STAT
    last = stage == len(STAGES) - 1
    held = [
        jax.ShapeDtypeStruct((NX, rows, ALL), jnp.bfloat16),
        jax.ShapeDtypeStruct((HEADS, NX * TOK, DH), jnp.float32),
    ]
    message = jax.ShapeDtypeStruct((rows, len(heads) * DH), jnp.bfloat16)
    if stage == 0:
        arrays = [*queries, *pieces]
        in_specs = [any_space] * len(arrays)
        out_shape = [jax.ShapeDtypeStruct((NX, TOK, ALL), jnp.bfloat16), *held]
        aliases = {}
    else:
        arrays = [queries, *before, *pieces]
        in_specs = [in_vmem] * 3 + [any_space] * len(pieces)
        out_shape = held + [message] * (NX if last else 0)
        aliases = {2: 0, 3: 1}
    return pl.pallas_call(
        functools.partial(attend_kernel, stage, heads),
        out_shape=out_shape,
        in_specs=[in_smem] + in_specs,
        out_specs=[in_vmem] * len(out_shape),
        input_output_aliases=aliases,
        scratch_shapes=[
            pltpu.VMEM((slots, 2, TOK, ALL), jnp.bfloat16),
            pltpu.VMEM((len(heads), slots, BLK, TOK), jnp.float32),
            pltpu.SemaphoreType.DMA((NX + 6,)),
        ],
        compiler_params=pltpu.CompilerParams(vmem_limit_bytes=VMEM),
        cost_estimate=pl.CostEstimate(
            flops=8_000_000_000, bytes_accessed=24_000_000, transcendentals=4_000_000
        ),
    )(plan, *arrays)


def join_kernel(*refs):
    shares, out = refs[:-1], refs[-1]
    eye = lax.broadcasted_iota(jnp.int32, (DH, DH), 0) == lax.broadcasted_iota(
        jnp.int32, (DH, DH), 1
    )
    for h in range(PAIR):
        cols = slice(h * DH, (h + 1) * DH)
        stats = []
        for share in shares:
            terms = share[TOK : TOK + STAT, cols].astype(jnp.float32)
            stats.append(terms[0:4] + terms[4:8] + terms[8:12])
        for t in range(TOK // DH):
            lse = [
                jnp.sum(
                    jnp.where(eye, jnp.broadcast_to(s[t : t + 1], (DH, DH)), 0.0),
                    axis=1,
                    keepdims=True,
                )
                for s in stats
            ]
            top = functools.reduce(jnp.maximum, lse)
            scale = [jnp.exp(v - top) for v in lse]
            norm = functools.reduce(jnp.add, scale)
            rows = slice(t * DH, (t + 1) * DH)
            terms = [f * s[rows, cols].astype(jnp.float32) for f, s in zip(scale, shares)]
            out[rows, cols] = (functools.reduce(jnp.add, terms) / norm).astype(jnp.bfloat16)


def join(messages):
    return pl.pallas_call(
        join_kernel,
        out_shape=jax.ShapeDtypeStruct((TOK, WIDE), jnp.bfloat16),
        in_specs=[in_vmem] * len(messages),
        out_specs=in_vmem,
        compiler_params=pltpu.CompilerParams(vmem_limit_bytes=VMEM),
        cost_estimate=pl.CostEstimate(
            flops=4_000_000, bytes_accessed=1_300_000, transcendentals=8_000
        ),
    )(*messages)


def project_kernel(chunk, *refs):
    att, weight, rest, out = refs[:NY], refs[NY : 2 * NY], refs[2 * NY : -1], refs[-1]
    width = TILE
    cols = pl.ds(pl.multiple_of(pl.program_id(0) * width, width), width)
    rows = slice(chunk * WIDE, (chunk + 1) * WIDE)
    terms = [
        jnp.dot(a[...], w[rows, cols], preferred_element_type=jnp.float32)
        for a, w in zip(att, weight)
    ]
    total = functools.reduce(jnp.add, terms)
    if rest:
        out[...] = (total + rest[0][:, cols]).astype(out.dtype)
    else:
        out[:, cols] = total


def project(chunk, att, weight, so_far=()):
    columns = weight[0].shape[1]
    dtype = jnp.bfloat16 if so_far else jnp.float32
    tiled = pl.BlockSpec((TOK, TILE), lambda j: (0, j))
    return pl.pallas_call(
        functools.partial(project_kernel, chunk),
        grid=(columns // TILE,),
        out_shape=jax.ShapeDtypeStruct((TOK, columns), dtype),
        in_specs=[in_vmem] * (2 * NY + len(so_far)),
        out_specs=tiled if so_far else in_vmem,
        compiler_params=pltpu.CompilerParams(vmem_limit_bytes=VMEM),
        cost_estimate=pl.CostEstimate(
            flops=1_073_741_824, bytes_accessed=5_000_000, transcendentals=0
        ),
    )(*att, *weight, *so_far)


def ring_step(right, left):
    return (
        lax.ppermute(right, "z", shift(NZ, 1)),
        lax.ppermute(left, "z", shift(NZ, -1)),
    )


def after(value, *others):
    return lax.optimization_barrier((value, others))[0]


def body(queries, key_value, out_weight, random_blocks, global_ids):
    z, x, y = lax.axis_index("z"), lax.axis_index("x"), lax.axis_index("head")
    own = jnp.transpose(key_value, (1, 0, 2))
    place = jnp.stack([z, x]).astype(jnp.int32)
    first = ring_step(own, own)
    plane = [queries] + [lax.ppermute(queries, "x", shift(NX, s)) for s in range(1, NX)]
    plan = make_plan(random_blocks.reshape(-1), global_ids, place)
    columns = out_weight.shape[1] // NY
    weight = [
        lax.dynamic_slice_in_dim(out_weight, ((y + s) % NY) * columns, columns, axis=1)
        for s in range(NY)
    ]
    second = ring_step(*(after(f, plan, weight) for f in first))
    w1, w3 = (lax.ppermute(after(weight[s], plane), "head", shift(NY, s)) for s in (1, 3))
    third = ring_step(*(after(f, plane) for f in second))
    near = [own, first[1], second[1], second[0], first[0]]
    plane, *held = attend(0, plan, plane, near)
    third = [after(f, held, w1, w3) for f in third]
    w2 = lax.ppermute(after(weight[2], w1, w3), "head", shift(NY, 2))
    fourth = ring_step(third[0][0], third[1][1])
    held = attend(1, plan, plane, [third[1], third[0]], held)
    held = after(held, w2)
    weight = [weight[0], w1, w2, w3]
    so_far, back = (), ()
    for c in range(HEADS // PAIR):
        heads = tuple(range(c * PAIR, (c + 1) * PAIR))
        *held, m0, m1, m2, m3 = attend(2, plan, plane, fourth, held, heads)
        m1, m2, m3 = after((m1, m2, m3), *back[::2])
        back = [lax.ppermute(m, "x", shift(NX, -s)) for s, m in ((1, m1), (2, m2), (3, m3))]
        att = join([m0, *back])
        everyone = [att] + [lax.ppermute(att, "head", shift(NY, s)) for s in range(1, NY)]
        so_far = (project(c, everyone, weight, so_far),)
    return so_far[0]


def solution(mesh):
    devices = mesh.devices.reshape(mesh.devices.shape[0], NZ, NX, NY)
    grid = Mesh(devices, ("batch", "z", "x", "head"))
    rows = ("batch", "z", "x")
    in_specs = (
        P(rows, "head"),
        P(rows, None, "head"),
        P("head", None),
        P("batch", None),
        P("batch"),
    )
    return jax.shard_map(
        body, mesh=grid, in_specs=in_specs, out_specs=P(rows, "head"), check_vma=False
    )
```

```python
import functools
import math

import jax
import jax.numpy as jnp
from jax import lax
from jax.experimental import pallas as pl
from jax.experimental.pallas import tpu as pltpu
from jax.sharding import Mesh
from jax.sharding import PartitionSpec as P

DH = 128
BLK = 64
NEG = -1e30
NZ = 8
NX = 4
NY = 4
BPD = 8
TOK = BLK * BPD
HEADS = 4
ALL = HEADS * DH
PAIR = 2
WIDE = PAIR * DH
STAT = 16
CHAINS = 16
TILE = 256
QBS = NX * BPD
COUNT, LISTED, ORDER = QBS, QBS * 8 + 8, QBS + 8
INDEX_AT = 2 * COUNT
ORDER_AT = INDEX_AT + 2 * LISTED
DENSE_AT = ORDER_AT + 2 * ORDER
X_AT = DENSE_AT + 2
PLAN = X_AT + 1
STAGES = ((0, 1, 2, 6, 7), (3, 5), (4,))
SLOTS = [stage * 8 + part.index(p) for p in range(8) for stage, part in enumerate(STAGES) if p in part]
COUNT, LISTED, ORDER = QBS, QBS * 8 + 8, QBS + 8
INDEX_AT = len(STAGES) * COUNT
ORDER_AT = INDEX_AT + len(STAGES) * LISTED
DENSE_AT = ORDER_AT + len(STAGES) * ORDER
X_AT = DENSE_AT + 2
PLAN = X_AT + 1
SCALE = 1.0 / math.sqrt(DH)
SCALE2 = SCALE / math.log(2.0)
VMEM = 20 * 1024 * 1024

any_space = pl.BlockSpec(memory_space=pl.ANY)
in_vmem = pl.BlockSpec(memory_space=pltpu.VMEM)
in_smem = pl.BlockSpec(memory_space=pltpu.SMEM)


def shift(count, by):
    return [(i, (i + by) % count) for i in range(count)]


def plan_kernel(table, glob, place, slots, plan):
    z, x = place[0], place[1]
    plan[X_AT] = x
    for g in range(2):
        owner = glob[g] >> 3
        slot = (x - (owner & 3)) & 3
        plan[DENSE_AT + g] = jnp.where((owner >> 2) == z, slot * BPD + (glob[g] & 7), -1)

    def one(qb, carry):
        qx = (x - (qb >> 3)) & 3
        block = ((z * NX + qx) << 3) + (qb & 7)
        entries = [(block - 1, block > 0), (block, None)]
        entries += [(block + 1, block < NZ * NX * BPD - 1)]
        entries += [(glob[0], None), (glob[1], None)]
        entries += [(table[block * 3 + j], None) for j in range(3)]
        for stage in range(len(STAGES)):
            plan[stage * COUNT + qb] = 0
            for k in range(8):
                plan[INDEX_AT + stage * LISTED + qb * 8 + k] = 0
        for key, exists in entries:
            key = jnp.clip(key, 0, NZ * NX * BPD - 1)
            owner = key >> 3
            here = (owner & 3) == x
            if exists is not None:
                here = here & exists
            slot = slots[((owner >> 2) - z) & 7]
            stage, slot = slot >> 3, slot & 7
            filled = plan[stage * COUNT + qb]
            plan[INDEX_AT + stage * LISTED + qb * 8 + filled] = (slot << 3) + (key & 7)
            plan[stage * COUNT + qb] = filled + here.astype(jnp.int32)
        is_global = (block == glob[0]) | (block == glob[1])
        for stage in range(len(STAGES)):
            plan[stage * COUNT + qb] = jnp.where(is_global, 0, plan[stage * COUNT + qb])
        return carry

    lax.fori_loop(0, QBS, one, 0)

    def place_one(stage, pairs, qb, filled):
        plan[filled] = qb
        return filled + (((plan[stage * COUNT + qb] + 1) >> 1) == pairs).astype(jnp.int32)

    for stage in range(len(STAGES)):
        filled = jnp.int32(ORDER_AT + stage * ORDER)
        for pairs in range(4, -1, -1):
            filled = lax.fori_loop(0, QBS, functools.partial(place_one, stage, pairs), filled)


def make_plan(table, glob, place):
    return pl.pallas_call(
        plan_kernel,
        out_shape=jax.ShapeDtypeStruct((PLAN,), jnp.int32),
        in_specs=[in_smem] * 4,
        out_specs=in_smem,
        compiler_params=pltpu.CompilerParams(vmem_limit_bytes=1024 * 1024),
    )(table, glob, place, jnp.array(SLOTS, jnp.int32))


def dot_t(a, b):
    return lax.dot_general(a, b, (((1,), (1,)), ((), ())), preferred_element_type=jnp.float32)


def attend_kernel(stage, heads, *refs):
    plan = refs[0]
    at_once = CHAINS // len(heads)
    kv_s, wide, sems = refs[-3:]
    slots = kv_s.shape[0]
    last = stage == len(STAGES) - 1
    if stage == 0:
        q_s, o_s, stat = refs[-6:-3]
        copies = [(refs[1 + s], q_s.at[s]) for s in range(NX)]
        at_ref = 1 + NX
    else:
        q_s = refs[1]
        copies, at_ref = [], 4
        outs = refs[-9:-3] if last else refs[-5:-3]
        o_s, stat = outs[:2]
    for slot, piece in enumerate(STAGES[stage]):
        if piece == NZ // 2:
            copies += [(refs[at_ref + k], kv_s.at[slot, k]) for k in range(2)]
        else:
            copies.append((refs[at_ref], kv_s.at[slot]))
        at_ref += 1
    cols = pl.ds(heads[0] * DH, len(heads) * DH)
    out = [(o_s.at[s, :, cols], outs[2 + s]) for s in range(NX)] if last else []
    copies = [pltpu.make_async_copy(a, b, sems.at[n]) for n, (a, b) in enumerate(copies)]
    for copy in copies:
        copy.start()
    for copy in copies:
        copy.wait()

    def share(top, both):
        total = both[:, DH:]
        return both[:, :DH] / total, top * SCALE + jnp.log(total)

    def at(qb, head):
        rows = pl.ds(pl.multiple_of((qb & 7) * BLK, BLK), BLK)
        return (qb >> 3, rows, slice(head * DH, (head + 1) * DH)), (
            head,
            pl.ds(pl.multiple_of(qb * BLK, BLK), BLK),
            slice(None),
        )

    def merge(qb, head, part, lse):
        if stage == 0:
            return part.astype(jnp.bfloat16), lse
        here, line = at(qb, head)
        before = stat[line]
        top = jnp.maximum(before, lse)
        old, new = jnp.exp(before - top), jnp.exp(lse - top)
        both = old + new
        part = (o_s[here].astype(jnp.float32) * old + part * new) / both
        return part.astype(jnp.bfloat16), top + jnp.log(both)

    def finish(qb, head, part, lse):
        here, line = at(qb, head)
        o_s[here] = part
        stat[line] = lse

    def load_q(qb, head):
        rows = pl.ds(pl.multiple_of((qb & 7) * BLK, BLK), BLK)
        return q_s[qb >> 3, rows, head * DH : (head + 1) * DH]

    lane = lax.broadcasted_iota(jnp.int32, (BLK, 2 * BLK), 1)

    def group(g, pairs):
        blocks = [plan[ORDER_AT + stage * ORDER + g * at_once + i] for i in range(at_once)]
        counts = [plan[stage * COUNT + qb] for qb in blocks]
        where = []
        for i in range(at_once):
            first = INDEX_AT + stage * LISTED + blocks[i] * 8
            entries = [plan[first + e] for e in range(2 * pairs)]
            where.append(
                [(e >> 3, pl.ds(pl.multiple_of((e & 7) * BLK, BLK), BLK)) for e in entries]
            )

        def load(i, h, t, kind):
            cols = slice(h * DH, (h + 1) * DH)
            both = [kv_s[piece, kind, rows, cols] for piece, rows in where[i][2 * t : 2 * t + 2]]
            return jnp.concatenate(both, axis=0)

        chains = [(i, h) for i in range(at_once) for h in heads]
        queries = [load_q(blocks[i], h) for i, h in chains]
        scores = [
            [
                jnp.where(
                    lane < (counts[i] - 2 * t) * BLK, dot_t(query, load(i, h, t, 0)), NEG
                )
                for t in range(pairs)
            ]
            for query, (i, h) in zip(queries, chains)
        ]
        tops = [
            jnp.max(functools.reduce(jnp.maximum, tiles), axis=1, keepdims=True)
            for tiles in scores
        ]
        weights = [
            [jnp.exp2((tile - top) * SCALE2).astype(jnp.bfloat16) for tile in tiles]
            for tiles, top in zip(scores, tops)
        ]
        sums = []
        for (i, h), tiles in zip(chains, weights):
            both = None
            for t in range(pairs):
                values = load(i, h, t, 1)
                values = jnp.concatenate([values, jnp.ones_like(values)], axis=1)
                term = jnp.dot(tiles[t], values, preferred_element_type=jnp.float32)
                both = term if both is None else both + term
            sums.append(both)
        shares = [share(top, both) for top, both in zip(tops, sums)]
        merged = [
            merge(blocks[i], h, part, jnp.where(counts[i] > 0, lse, NEG))
            for (i, h), (part, lse) in zip(chains, shares)
        ]
        for (i, h), (part, lse) in zip(chains, merged):
            finish(blocks[i], h, part, lse)

    def nothing(g):
        for i in range(at_once):
            qb = plan[ORDER_AT + stage * ORDER + g * at_once + i]
            for h in heads:
                finish(
                    qb, h, jnp.zeros((BLK, DH), jnp.bfloat16), jnp.full((BLK, DH), NEG, jnp.float32)
                )

    def any_group(g, carry):
        most = (plan[stage * COUNT + plan[ORDER_AT + stage * ORDER + g * at_once]] + 1) >> 1
        if stage == 0:
            pl.when(most == 0)(functools.partial(nothing, g))
        for pairs in range(1, 5):
            pl.when(most == pairs)(functools.partial(group, g, pairs))
        return carry

    lax.fori_loop(0, QBS // at_once, any_group, 0)

    for g in range(2):

        @pl.when(plan[DENSE_AT + g] >= 0)
        def _(g=g):
            qb = plan[DENSE_AT + g]
            queries = [load_q(qb, h) for h in heads]

            def score(p, tops):
                tiles = [
                    dot_t(query, kv_s[p, 0, :, h * DH : (h + 1) * DH])
                    for query, h in zip(queries, heads)
                ]
                for n, tile in enumerate(tiles):
                    wide[n, p] = tile
                parts = [
                    [tile[:, t * DH : (t + 1) * DH] for t in range(TOK // DH)] for tile in tiles
                ]
                return tuple(
                    functools.reduce(jnp.maximum, part, top) for part, top in zip(parts, tops)
                )

            low = jnp.full((BLK, DH), NEG, jnp.float32)
            tops = lax.fori_loop(0, slots, score, (low,) * len(heads))
            tops = [jnp.max(top, axis=1, keepdims=True) for top in tops]

            def gather(p, sums):
                done = []
                for n, h in enumerate(heads):
                    weights = jnp.exp2((wide[n, p] - tops[n]) * SCALE2).astype(jnp.bfloat16)
                    values = kv_s[p, 1, :, h * DH : (h + 1) * DH]
                    values = jnp.concatenate([values, jnp.ones_like(values)], axis=1)
                    done.append(
                        sums[n] + jnp.dot(weights, values, preferred_element_type=jnp.float32)
                    )
                return tuple(done)

            none = jnp.zeros((BLK, 2 * DH), jnp.float32)
            sums = lax.fori_loop(0, slots, gather, (none,) * len(heads))
            for n, h in enumerate(heads):
                finish(qb, h, *merge(qb, h, *share(tops[n], sums[n])))

    eye = lax.broadcasted_iota(jnp.int32, (DH, DH), 0) == lax.broadcasted_iota(
        jnp.int32, (DH, DH), 1
    )
    for s in range(NX if last else 0):
        for h in heads:
            lines = []
            for t in range(TOK // DH):
                tile = stat[h, s * TOK + t * DH : s * TOK + (t + 1) * DH, :]
                lines.append(jnp.sum(jnp.where(eye, tile, 0.0), axis=0, keepdims=True))
            left = jnp.concatenate(lines, axis=0)
            terms = []
            for _ in range(3):
                term = left.astype(jnp.bfloat16).astype(jnp.float32)
                terms.append(term)
                left = left - term
            terms.append(jnp.zeros_like(left))
            o_s[s, TOK : TOK + STAT, h * DH : (h + 1) * DH] = jnp.concatenate(
                terms, axis=0
            ).astype(jnp.bfloat16)
    back = [pltpu.make_async_copy(a, b, sems.at[n]) for n, (a, b) in enumerate(out)]
    for copy in back:
        copy.start()
    for copy in back:
        copy.wait()


def attend(stage, plan, queries, pieces, before=(), heads=tuple(range(HEADS))):
    slots = len(STAGES[stage])
    rows = TOK + STAT
    last = stage == len(STAGES) - 1
    held = [
        jax.ShapeDtypeStruct((NX, rows, ALL), jnp.bfloat16),
        jax.ShapeDtypeStruct((HEADS, NX * TOK, DH), jnp.float32),
    ]
    message = jax.ShapeDtypeStruct((rows, len(heads) * DH), jnp.bfloat16)
    if stage == 0:
        arrays = [*queries, *pieces]
        in_specs = [any_space] * len(arrays)
        out_shape = [jax.ShapeDtypeStruct((NX, TOK, ALL), jnp.bfloat16), *held]
        aliases = {}
    else:
        arrays = [queries, *before, *pieces]
        in_specs = [in_vmem] * 3 + [any_space] * len(pieces)
        out_shape = held + [message] * (NX if last else 0)
        aliases = {2: 0, 3: 1}
    return pl.pallas_call(
        functools.partial(attend_kernel, stage, heads),
        out_shape=out_shape,
        in_specs=[in_smem] + in_specs,
        out_specs=[in_vmem] * len(out_shape),
        input_output_aliases=aliases,
        scratch_shapes=[
            pltpu.VMEM((slots, 2, TOK, ALL), jnp.bfloat16),
            pltpu.VMEM((len(heads), slots, BLK, TOK), jnp.float32),
            pltpu.SemaphoreType.DMA((NX + 6,)),
        ],
        compiler_params=pltpu.CompilerParams(vmem_limit_bytes=VMEM),
        cost_estimate=pl.CostEstimate(
            flops=8_000_000_000, bytes_accessed=24_000_000, transcendentals=4_000_000
        ),
    )(plan, *arrays)


def join_kernel(*refs):
    shares, out = refs[:-1], refs[-1]
    eye = lax.broadcasted_iota(jnp.int32, (DH, DH), 0) == lax.broadcasted_iota(
        jnp.int32, (DH, DH), 1
    )
    for h in range(PAIR):
        cols = slice(h * DH, (h + 1) * DH)
        stats = []
        for share in shares:
            terms = share[TOK : TOK + STAT, cols].astype(jnp.float32)
            stats.append(terms[0:4] + terms[4:8] + terms[8:12])
        for t in range(TOK // DH):
            lse = [
                jnp.sum(
                    jnp.where(eye, jnp.broadcast_to(s[t : t + 1], (DH, DH)), 0.0),
                    axis=1,
                    keepdims=True,
                )
                for s in stats
            ]
            top = functools.reduce(jnp.maximum, lse)
            scale = [jnp.exp(v - top) for v in lse]
            norm = functools.reduce(jnp.add, scale)
            rows = slice(t * DH, (t + 1) * DH)
            terms = [f * s[rows, cols].astype(jnp.float32) for f, s in zip(scale, shares)]
            out[rows, cols] = (functools.reduce(jnp.add, terms) / norm).astype(jnp.bfloat16)


def join(messages):
    return pl.pallas_call(
        join_kernel,
        out_shape=jax.ShapeDtypeStruct((TOK, WIDE), jnp.bfloat16),
        in_specs=[in_vmem] * len(messages),
        out_specs=in_vmem,
        compiler_params=pltpu.CompilerParams(vmem_limit_bytes=VMEM),
        cost_estimate=pl.CostEstimate(
            flops=4_000_000, bytes_accessed=1_300_000, transcendentals=8_000
        ),
    )(*messages)


def project_kernel(chunk, *refs):
    att, weight, rest, out = refs[:NY], refs[NY : 2 * NY], refs[2 * NY : -1], refs[-1]
    width = TILE
    cols = pl.ds(pl.multiple_of(pl.program_id(0) * width, width), width)
    rows = slice(chunk * WIDE, (chunk + 1) * WIDE)
    terms = [
        jnp.dot(a[...], w[rows, cols], preferred_element_type=jnp.float32)
        for a, w in zip(att, weight)
    ]
    total = functools.reduce(jnp.add, terms)
    if rest:
        out[...] = (total + rest[0][:, cols]).astype(out.dtype)
    else:
        out[:, cols] = total


def project(chunk, att, weight, so_far=()):
    columns = weight[0].shape[1]
    dtype = jnp.bfloat16 if so_far else jnp.float32
    tiled = pl.BlockSpec((TOK, TILE), lambda j: (0, j))
    return pl.pallas_call(
        functools.partial(project_kernel, chunk),
        grid=(columns // TILE,),
        out_shape=jax.ShapeDtypeStruct((TOK, columns), dtype),
        in_specs=[in_vmem] * (2 * NY + len(so_far)),
        out_specs=tiled if so_far else in_vmem,
        compiler_params=pltpu.CompilerParams(vmem_limit_bytes=VMEM),
        cost_estimate=pl.CostEstimate(
            flops=1_073_741_824, bytes_accessed=5_000_000, transcendentals=0
        ),
    )(*att, *weight, *so_far)


def ring_step(right, left):
    return (
        lax.ppermute(right, "z", shift(NZ, 1)),
        lax.ppermute(left, "z", shift(NZ, -1)),
    )


def after(value, *others):
    return lax.optimization_barrier((value, others))[0]


def body(queries, key_value, out_weight, random_blocks, global_ids):
    z, x, y = lax.axis_index("z"), lax.axis_index("x"), lax.axis_index("head")
    own = jnp.transpose(key_value, (1, 0, 2))
    place = jnp.stack([z, x]).astype(jnp.int32)
    first = ring_step(own, own)
    plane = [queries] + [lax.ppermute(queries, "x", shift(NX, s)) for s in range(1, NX)]
    plan = make_plan(random_blocks.reshape(-1), global_ids, place)
    columns = out_weight.shape[1] // NY
    weight = [
        lax.dynamic_slice_in_dim(out_weight, ((y + s) % NY) * columns, columns, axis=1)
        for s in range(NY)
    ]
    second = ring_step(*(after(f, plan, weight) for f in first))
    w1, w3 = (lax.ppermute(after(weight[s], plane), "head", shift(NY, s)) for s in (1, 3))
    third = ring_step(*(after(f, plane) for f in second))
    near = [own, first[1], second[1], second[0], first[0]]
    plane, *held = attend(0, plan, plane, near)
    third = [after(f, held, w1, w3) for f in third]
    w2 = lax.ppermute(after(weight[2], w1, w3), "head", shift(NY, 2))
    fourth = ring_step(third[0][0], third[1][1])
    held = attend(1, plan, plane, [third[1], third[0]], held)
    held = after(held, w2)
    weight = [weight[0], w1, w2, w3]
    so_far, back = (), ()
    for c in range(HEADS // PAIR):
        heads = tuple(range(c * PAIR, (c + 1) * PAIR))
        *held, m0, m1, m2, m3 = attend(2, plan, plane, fourth, held, heads)
        m1, m2, m3 = after((m1, m2, m3), *back[:1])
        back = [lax.ppermute(m, "x", shift(NX, -s)) for s, m in ((2, m2), (1, m1), (3, m3))]
        att = join([m0, *back])
        a1, a3, a2 = (lax.ppermute(att, "head", shift(NY, s)) for s in (1, 3, 2))
        everyone = [att, a1, a2, a3]
        so_far = (project(c, everyone, weight, so_far),)
    return so_far[0]


def solution(mesh):
    devices = mesh.devices.reshape(mesh.devices.shape[0], NZ, NX, NY)
    grid = Mesh(devices, ("batch", "z", "x", "head"))
    rows = ("batch", "z", "x")
    in_specs = (
        P(rows, "head"),
        P(rows, None, "head"),
        P("head", None),
        P("batch", None),
        P("batch"),
    )
    return jax.shard_map(
        body, mesh=grid, in_specs=in_specs, out_specs=P(rows, "head"), check_vma=False
    )
```

```python
import functools
import math

import jax
import jax.numpy as jnp
from jax import lax
from jax.experimental import pallas as pl
from jax.experimental.pallas import tpu as pltpu
from jax.sharding import Mesh
from jax.sharding import PartitionSpec as P

DH = 128
BLK = 64
NEG = -1e30
NZ = 8
NX = 4
NY = 4
BPD = 8
TOK = BLK * BPD
HEADS = 4
ALL = HEADS * DH
PAIR = 2
WIDE = PAIR * DH
STAT = 16
CHAINS = 16
TILE = 256
QBS = NX * BPD
COUNT, LISTED, ORDER = QBS, QBS * 8 + 8, QBS + 8
INDEX_AT = 2 * COUNT
ORDER_AT = INDEX_AT + 2 * LISTED
DENSE_AT = ORDER_AT + 2 * ORDER
X_AT = DENSE_AT + 2
PLAN = X_AT + 1
STAGES = ((0, 1, 2, 6, 7), (3, 5), (4,))
SLOTS = [stage * 8 + part.index(p) for p in range(8) for stage, part in enumerate(STAGES) if p in part]
COUNT, LISTED, ORDER = QBS, QBS * 8 + 8, QBS + 8
INDEX_AT = len(STAGES) * COUNT
ORDER_AT = INDEX_AT + len(STAGES) * LISTED
DENSE_AT = ORDER_AT + len(STAGES) * ORDER
X_AT = DENSE_AT + 2
PLAN = X_AT + 1
SCALE = 1.0 / math.sqrt(DH)
SCALE2 = SCALE / math.log(2.0)
VMEM = 20 * 1024 * 1024

any_space = pl.BlockSpec(memory_space=pl.ANY)
in_vmem = pl.BlockSpec(memory_space=pltpu.VMEM)
in_smem = pl.BlockSpec(memory_space=pltpu.SMEM)


def shift(count, by):
    return [(i, (i + by) % count) for i in range(count)]


def plan_kernel(table, glob, place, slots, plan):
    z, x = place[0], place[1]
    plan[X_AT] = x
    for g in range(2):
        owner = glob[g] >> 3
        slot = (x - (owner & 3)) & 3
        plan[DENSE_AT + g] = jnp.where((owner >> 2) == z, slot * BPD + (glob[g] & 7), -1)

    def one(qb, carry):
        qx = (x - (qb >> 3)) & 3
        block = ((z * NX + qx) << 3) + (qb & 7)
        entries = [(block - 1, block > 0), (block, None)]
        entries += [(block + 1, block < NZ * NX * BPD - 1)]
        entries += [(glob[0], None), (glob[1], None)]
        entries += [(table[block * 3 + j], None) for j in range(3)]
        for stage in range(len(STAGES)):
            plan[stage * COUNT + qb] = 0
            for k in range(8):
                plan[INDEX_AT + stage * LISTED + qb * 8 + k] = 0
        for key, exists in entries:
            key = jnp.clip(key, 0, NZ * NX * BPD - 1)
            owner = key >> 3
            here = (owner & 3) == x
            if exists is not None:
                here = here & exists
            slot = slots[((owner >> 2) - z) & 7]
            stage, slot = slot >> 3, slot & 7
            filled = plan[stage * COUNT + qb]
            plan[INDEX_AT + stage * LISTED + qb * 8 + filled] = (slot << 3) + (key & 7)
            plan[stage * COUNT + qb] = filled + here.astype(jnp.int32)
        is_global = (block == glob[0]) | (block == glob[1])
        for stage in range(len(STAGES)):
            plan[stage * COUNT + qb] = jnp.where(is_global, 0, plan[stage * COUNT + qb])
        return carry

    lax.fori_loop(0, QBS, one, 0)

    def place_one(stage, pairs, qb, filled):
        plan[filled] = qb
        return filled + (((plan[stage * COUNT + qb] + 1) >> 1) == pairs).astype(jnp.int32)

    for stage in range(len(STAGES)):
        filled = jnp.int32(ORDER_AT + stage * ORDER)
        for pairs in range(4, -1, -1):
            filled = lax.fori_loop(0, QBS, functools.partial(place_one, stage, pairs), filled)


def make_plan(table, glob, place):
    return pl.pallas_call(
        plan_kernel,
        out_shape=jax.ShapeDtypeStruct((PLAN,), jnp.int32),
        in_specs=[in_smem] * 4,
        out_specs=in_smem,
        compiler_params=pltpu.CompilerParams(vmem_limit_bytes=1024 * 1024),
    )(table, glob, place, jnp.array(SLOTS, jnp.int32))


def dot_t(a, b):
    return lax.dot_general(a, b, (((1,), (1,)), ((), ())), preferred_element_type=jnp.float32)


def attend_kernel(stage, heads, *refs):
    plan = refs[0]
    at_once = CHAINS // len(heads)
    kv_s, wide, sems = refs[-3:]
    slots = kv_s.shape[0]
    last = stage == len(STAGES) - 1
    if stage == 0:
        q_s, o_s, stat = refs[-6:-3]
        copies = [(refs[1 + s], q_s.at[s]) for s in range(NX)]
        at_ref = 1 + NX
    else:
        q_s = refs[1]
        copies, at_ref = [], 4
        outs = refs[-9:-3] if last else refs[-5:-3]
        o_s, stat = outs[:2]
    for slot, piece in enumerate(STAGES[stage]):
        if piece == NZ // 2:
            copies += [(refs[at_ref + k], kv_s.at[slot, k]) for k in range(2)]
        else:
            lanes = pl.ds(heads[0] * DH, len(heads) * DH)
            copies.append((refs[at_ref].at[:, :, lanes], kv_s.at[slot]))
        at_ref += 1
    cols = pl.ds(heads[0] * DH, len(heads) * DH)
    out = [(o_s.at[s, :, cols], outs[2 + s]) for s in range(NX)] if last else []
    copies = [pltpu.make_async_copy(a, b, sems.at[n]) for n, (a, b) in enumerate(copies)]
    for copy in copies:
        copy.start()
    for copy in copies:
        copy.wait()

    def share(top, both):
        total = both[:, DH:]
        return both[:, :DH] / total, top * SCALE + jnp.log(total)

    def at(qb, head):
        rows = pl.ds(pl.multiple_of((qb & 7) * BLK, BLK), BLK)
        return (qb >> 3, rows, slice(head * DH, (head + 1) * DH)), (
            head,
            pl.ds(pl.multiple_of(qb * BLK, BLK), BLK),
            slice(None),
        )

    def merge(qb, head, part, lse):
        if stage == 0:
            return part.astype(jnp.bfloat16), lse
        here, line = at(qb, head)
        before = stat[line]
        top = jnp.maximum(before, lse)
        old, new = jnp.exp(before - top), jnp.exp(lse - top)
        both = old + new
        part = (o_s[here].astype(jnp.float32) * old + part * new) / both
        return part.astype(jnp.bfloat16), top + jnp.log(both)

    def finish(qb, head, part, lse):
        here, line = at(qb, head)
        o_s[here] = part
        stat[line] = lse

    def load_q(qb, head):
        rows = pl.ds(pl.multiple_of((qb & 7) * BLK, BLK), BLK)
        return q_s[qb >> 3, rows, head * DH : (head + 1) * DH]

    lane = lax.broadcasted_iota(jnp.int32, (BLK, 2 * BLK), 1)

    def group(g, pairs):
        blocks = [plan[ORDER_AT + stage * ORDER + g * at_once + i] for i in range(at_once)]
        counts = [plan[stage * COUNT + qb] for qb in blocks]
        where = []
        for i in range(at_once):
            first = INDEX_AT + stage * LISTED + blocks[i] * 8
            entries = [plan[first + e] for e in range(2 * pairs)]
            where.append(
                [(e >> 3, pl.ds(pl.multiple_of((e & 7) * BLK, BLK), BLK)) for e in entries]
            )

        def load(i, h, t, kind):
            cols = slice((h - heads[0]) * DH, (h - heads[0] + 1) * DH)
            both = [kv_s[piece, kind, rows, cols] for piece, rows in where[i][2 * t : 2 * t + 2]]
            return jnp.concatenate(both, axis=0)

        chains = [(i, h) for i in range(at_once) for h in heads]
        queries = [load_q(blocks[i], h) for i, h in chains]
        scores = [
            [
                jnp.where(
                    lane < (counts[i] - 2 * t) * BLK, dot_t(query, load(i, h, t, 0)), NEG
                )
                for t in range(pairs)
            ]
            for query, (i, h) in zip(queries, chains)
        ]
        tops = [
            jnp.max(functools.reduce(jnp.maximum, tiles), axis=1, keepdims=True)
            for tiles in scores
        ]
        weights = [
            [jnp.exp2((tile - top) * SCALE2).astype(jnp.bfloat16) for tile in tiles]
            for tiles, top in zip(scores, tops)
        ]
        sums = []
        for (i, h), tiles in zip(chains, weights):
            both = None
            for t in range(pairs):
                values = load(i, h, t, 1)
                values = jnp.concatenate([values, jnp.ones_like(values)], axis=1)
                term = jnp.dot(tiles[t], values, preferred_element_type=jnp.float32)
                both = term if both is None else both + term
            sums.append(both)
        shares = [share(top, both) for top, both in zip(tops, sums)]
        merged = [
            merge(blocks[i], h, part, jnp.where(counts[i] > 0, lse, NEG))
            for (i, h), (part, lse) in zip(chains, shares)
        ]
        for (i, h), (part, lse) in zip(chains, merged):
            finish(blocks[i], h, part, lse)

    def nothing(g):
        for i in range(at_once):
            qb = plan[ORDER_AT + stage * ORDER + g * at_once + i]
            for h in heads:
                finish(
                    qb, h, jnp.zeros((BLK, DH), jnp.bfloat16), jnp.full((BLK, DH), NEG, jnp.float32)
                )

    def any_group(g, carry):
        most = (plan[stage * COUNT + plan[ORDER_AT + stage * ORDER + g * at_once]] + 1) >> 1
        if stage == 0:
            pl.when(most == 0)(functools.partial(nothing, g))
        for pairs in range(1, 5):
            pl.when(most == pairs)(functools.partial(group, g, pairs))
        return carry

    lax.fori_loop(0, QBS // at_once, any_group, 0)

    for g in range(2):

        @pl.when(plan[DENSE_AT + g] >= 0)
        def _(g=g):
            qb = plan[DENSE_AT + g]
            queries = [load_q(qb, h) for h in heads]

            def score(p, tops):
                tiles = [
                    dot_t(query, kv_s[p, 0, :, n * DH : (n + 1) * DH])
                    for n, query in enumerate(queries)
                ]
                for n, tile in enumerate(tiles):
                    wide[n, p] = tile
                parts = [
                    [tile[:, t * DH : (t + 1) * DH] for t in range(TOK // DH)] for tile in tiles
                ]
                return tuple(
                    functools.reduce(jnp.maximum, part, top) for part, top in zip(parts, tops)
                )

            low = jnp.full((BLK, DH), NEG, jnp.float32)
            tops = lax.fori_loop(0, slots, score, (low,) * len(heads))
            tops = [jnp.max(top, axis=1, keepdims=True) for top in tops]

            def gather(p, sums):
                done = []
                for n in range(len(heads)):
                    weights = jnp.exp2((wide[n, p] - tops[n]) * SCALE2).astype(jnp.bfloat16)
                    values = kv_s[p, 1, :, n * DH : (n + 1) * DH]
                    values = jnp.concatenate([values, jnp.ones_like(values)], axis=1)
                    done.append(
                        sums[n] + jnp.dot(weights, values, preferred_element_type=jnp.float32)
                    )
                return tuple(done)

            none = jnp.zeros((BLK, 2 * DH), jnp.float32)
            sums = lax.fori_loop(0, slots, gather, (none,) * len(heads))
            for n, h in enumerate(heads):
                finish(qb, h, *merge(qb, h, *share(tops[n], sums[n])))

    eye = lax.broadcasted_iota(jnp.int32, (DH, DH), 0) == lax.broadcasted_iota(
        jnp.int32, (DH, DH), 1
    )
    for s in range(NX if last else 0):
        for h in heads:
            lines = []
            for t in range(TOK // DH):
                tile = stat[h, s * TOK + t * DH : s * TOK + (t + 1) * DH, :]
                lines.append(jnp.sum(jnp.where(eye, tile, 0.0), axis=0, keepdims=True))
            left = jnp.concatenate(lines, axis=0)
            terms = []
            for _ in range(3):
                term = left.astype(jnp.bfloat16).astype(jnp.float32)
                terms.append(term)
                left = left - term
            terms.append(jnp.zeros_like(left))
            o_s[s, TOK : TOK + STAT, h * DH : (h + 1) * DH] = jnp.concatenate(
                terms, axis=0
            ).astype(jnp.bfloat16)
    back = [pltpu.make_async_copy(a, b, sems.at[n]) for n, (a, b) in enumerate(out)]
    for copy in back:
        copy.start()
    for copy in back:
        copy.wait()


def attend(stage, plan, queries, pieces, before=(), heads=tuple(range(HEADS))):
    slots = len(STAGES[stage])
    rows = TOK + STAT
    last = stage == len(STAGES) - 1
    held = [
        jax.ShapeDtypeStruct((NX, rows, ALL), jnp.bfloat16),
        jax.ShapeDtypeStruct((HEADS, NX * TOK, DH), jnp.float32),
    ]
    message = jax.ShapeDtypeStruct((rows, len(heads) * DH), jnp.bfloat16)
    if stage == 0:
        arrays = [*queries, *pieces]
        in_specs = [any_space] * len(arrays)
        out_shape = [jax.ShapeDtypeStruct((NX, TOK, ALL), jnp.bfloat16), *held]
        aliases = {}
    else:
        arrays = [queries, *before, *pieces]
        in_specs = [in_vmem] * 3 + [any_space] * len(pieces)
        out_shape = held + [message] * (NX if last else 0)
        aliases = {2: 0, 3: 1}
    return pl.pallas_call(
        functools.partial(attend_kernel, stage, heads),
        out_shape=out_shape,
        in_specs=[in_smem] + in_specs,
        out_specs=[in_vmem] * len(out_shape),
        input_output_aliases=aliases,
        scratch_shapes=[
            pltpu.VMEM((slots, 2, TOK, len(heads) * DH), jnp.bfloat16),
            pltpu.VMEM((len(heads), slots, BLK, TOK), jnp.float32),
            pltpu.SemaphoreType.DMA((NX + 6,)),
        ],
        compiler_params=pltpu.CompilerParams(vmem_limit_bytes=VMEM),
        cost_estimate=pl.CostEstimate(
            flops=8_000_000_000, bytes_accessed=24_000_000, transcendentals=4_000_000
        ),
    )(plan, *arrays)


def join_kernel(*refs):
    shares, out = refs[:-1], refs[-1]
    eye = lax.broadcasted_iota(jnp.int32, (DH, DH), 0) == lax.broadcasted_iota(
        jnp.int32, (DH, DH), 1
    )
    for h in range(PAIR):
        cols = slice(h * DH, (h + 1) * DH)
        stats = []
        for share in shares:
            terms = share[TOK : TOK + STAT, cols].astype(jnp.float32)
            stats.append(terms[0:4] + terms[4:8] + terms[8:12])
        for t in range(TOK // DH):
            lse = [
                jnp.sum(
                    jnp.where(eye, jnp.broadcast_to(s[t : t + 1], (DH, DH)), 0.0),
                    axis=1,
                    keepdims=True,
                )
                for s in stats
            ]
            top = functools.reduce(jnp.maximum, lse)
            scale = [jnp.exp(v - top) for v in lse]
            norm = functools.reduce(jnp.add, scale)
            rows = slice(t * DH, (t + 1) * DH)
            terms = [f * s[rows, cols].astype(jnp.float32) for f, s in zip(scale, shares)]
            out[rows, cols] = (functools.reduce(jnp.add, terms) / norm).astype(jnp.bfloat16)


def join(messages):
    return pl.pallas_call(
        join_kernel,
        out_shape=jax.ShapeDtypeStruct((TOK, WIDE), jnp.bfloat16),
        in_specs=[in_vmem] * len(messages),
        out_specs=in_vmem,
        compiler_params=pltpu.CompilerParams(vmem_limit_bytes=VMEM),
        cost_estimate=pl.CostEstimate(
            flops=4_000_000, bytes_accessed=1_300_000, transcendentals=8_000
        ),
    )(*messages)


def project_kernel(chunk, *refs):
    att, weight, rest, out = refs[:NY], refs[NY : 2 * NY], refs[2 * NY : -1], refs[-1]
    width = TILE
    cols = pl.ds(pl.multiple_of(pl.program_id(0) * width, width), width)
    rows = slice(chunk * WIDE, (chunk + 1) * WIDE)
    terms = [
        jnp.dot(a[...], w[rows, cols], preferred_element_type=jnp.float32)
        for a, w in zip(att, weight)
    ]
    total = functools.reduce(jnp.add, terms)
    if rest:
        out[...] = (total + rest[0][:, cols]).astype(out.dtype)
    else:
        out[:, cols] = total


def project(chunk, att, weight, so_far=()):
    columns = weight[0].shape[1]
    dtype = jnp.bfloat16 if so_far else jnp.float32
    tiled = pl.BlockSpec((TOK, TILE), lambda j: (0, j))
    return pl.pallas_call(
        functools.partial(project_kernel, chunk),
        grid=(columns // TILE,),
        out_shape=jax.ShapeDtypeStruct((TOK, columns), dtype),
        in_specs=[in_vmem] * (2 * NY + len(so_far)),
        out_specs=tiled if so_far else in_vmem,
        compiler_params=pltpu.CompilerParams(vmem_limit_bytes=VMEM),
        cost_estimate=pl.CostEstimate(
            flops=1_073_741_824, bytes_accessed=5_000_000, transcendentals=0
        ),
    )(*att, *weight, *so_far)


def ring_step(right, left):
    return (
        lax.ppermute(right, "z", shift(NZ, 1)),
        lax.ppermute(left, "z", shift(NZ, -1)),
    )


def after(value, *others):
    return lax.optimization_barrier((value, others))[0]


def body(queries, key_value, out_weight, random_blocks, global_ids):
    z, x, y = lax.axis_index("z"), lax.axis_index("x"), lax.axis_index("head")
    own = jnp.transpose(key_value, (1, 0, 2))
    place = jnp.stack([z, x]).astype(jnp.int32)
    first = ring_step(own, own)
    plane = [queries] + [lax.ppermute(queries, "x", shift(NX, s)) for s in range(1, NX)]
    plan = make_plan(random_blocks.reshape(-1), global_ids, place)
    columns = out_weight.shape[1] // NY
    weight = [
        lax.dynamic_slice_in_dim(out_weight, ((y + s) % NY) * columns, columns, axis=1)
        for s in range(NY)
    ]
    second = ring_step(*(after(f, plan, weight) for f in first))
    w1, w3 = (lax.ppermute(after(weight[s], plane), "head", shift(NY, s)) for s in (1, 3))
    third = ring_step(*(after(f, plane) for f in second))
    near = [own, first[1], second[1], second[0], first[0]]
    plane, *held = attend(0, plan, plane, near)
    third = [after(f, held, w1, w3) for f in third]
    w2 = lax.ppermute(after(weight[2], w1, w3), "head", shift(NY, 2))
    fourth = []
    for c in range(HEADS // PAIR):
        cols = slice(c * WIDE, (c + 1) * WIDE)
        fourth.append(ring_step(third[0][0, :, cols], third[1][1, :, cols]))
    held = attend(1, plan, plane, [third[1], third[0]], held)
    held = after(held, w2)
    weight = [weight[0], w1, w2, w3]
    so_far, back = (), ()
    for c in range(HEADS // PAIR):
        heads = tuple(range(c * PAIR, (c + 1) * PAIR))
        *held, m0, m1, m2, m3 = attend(2, plan, plane, fourth[c], held, heads)
        m1, m2, m3 = after((m1, m2, m3), *back[:1])
        back = [lax.ppermute(m, "x", shift(NX, -s)) for s, m in ((2, m2), (1, m1), (3, m3))]
        att = join([m0, *back])
        everyone = [att] + [lax.ppermute(att, "head", shift(NY, s)) for s in range(1, NY)]
        so_far = (project(c, everyone, weight, so_far),)
    return so_far[0]


def solution(mesh):
    devices = mesh.devices.reshape(mesh.devices.shape[0], NZ, NX, NY)
    grid = Mesh(devices, ("batch", "z", "x", "head"))
    rows = ("batch", "z", "x")
    in_specs = (
        P(rows, "head"),
        P(rows, None, "head"),
        P("head", None),
        P("batch", None),
        P("batch"),
    )
    return jax.shard_map(
        body, mesh=grid, in_specs=in_specs, out_specs=P(rows, "head"), check_vma=False
    )
```
